32 devices in a mesh: case: 2 (over x), slab: 16 (over z, y, core).
Axes of the slice: x: 2, y: 2, z: 4, core: 2. Of those that a mesh axis runs over, the one named last changes fastest.
Arguments:
- density: float32 [64, 256, 256], P('slab', 'case'), may hold values from 0.2 to 1
- support: int32 [64, 256, 256], P('slab'), may hold values 0 or 1
- loads: int32 [4, 64, 256, 256], P('case', 'slab'), may hold values from 0 to 7
- load_table: float32 [8, 3], replicated, may hold values from -4 to 4
Outputs:
- displacement: float32 [4, 3, 64, 256, 256], P('case', None, 'slab')
- filtered: float32 [64, 256, 256], P('slab', 'case')
The draws below stay inside these ranges and needn't reach their ends.
All inputs are finite; a program needn't handle non-finite values. No bound on the sum of `support` on one device may be relied on, other than what follows from the above.
Results may differ from the reference program's by a relative error of at most 0.0001.
Values sent between devices are 32-bit elements; how exact they have to be, the bound alone decides.
No kernel may reach another device: no remote copies, remote signals or barrier semaphores. Data moves between devices by JAX's collectives and lax.ppermute only.
A program may use at most 128 MiB of HBM per device.

```python
import jax
import jax.numpy as jnp

NY = 256
NZ = 256
ITERS = 3
FSWEEPS = 4
DIRECTIONS = 8
LOADS = 4
NX = 64


def place_ends(entries, key, smallest, top_value):
    index_at = [jax.random.randint(jax.random.fold_in(key, axis), (), 0, length) for axis, length in enumerate(entries.shape)]
    longest = entries.shape.index(max(entries.shape))
    beside = index_at[:longest] + [(index_at[longest] + 1) % entries.shape[longest]] + index_at[longest + 1:]
    return entries.at[tuple(index_at)].set(smallest).at[tuple(beside)].set(top_value)


def level_of(own_key, extent, cuts, smallest, top_value):
    level = 1.0
    for position, blocks in cuts:
        draws = jax.random.uniform(jax.random.fold_in(jax.random.fold_in(own_key, 6), position), (blocks,), jnp.float32, smallest / len(cuts), top_value / len(cuts))
        level = level * jnp.repeat(jnp.exp(draws), extent[position] // blocks).reshape((-1,) + (1,) * (len(extent) - 1 - position))
    return level


def normal_values(rng, shape, scale, reach, held_as=jnp.bfloat16):
    return jnp.clip(scale * jax.random.normal(rng, shape, jnp.float32), -reach, reach).astype(held_as)


def setup_inputs(seed: int = 0) -> dict:
    splits = jax.random.split(jax.random.key(seed), 5)
    return {
        "density": jnp.clip(0.2 + 0.8 * jax.random.uniform(splits[0], (NX, NY, NZ), jnp.float32) ** level_of(splits[0], (NX, NY, NZ), ((0, 16), (1, 2)), -0.2, 0.2), 0.2, 1.0),
        "support": place_ends((jax.random.randint(splits[1], (NX, NY, NZ), 0, 8) < 1).astype(jnp.int32), jax.random.fold_in(splits[1], 1), 0, 1),
        "loads": place_ends(jax.random.randint(splits[2], (LOADS, NX, NY, NZ), 0, DIRECTIONS), jax.random.fold_in(splits[2], 1), 0, DIRECTIONS - 1).astype(jnp.int32),
        "load_table": normal_values(splits[3], (DIRECTIONS, 3), 1.0, 4.0, jnp.float32),
    }


E_MIN = 1e-3
PENALTY = 3.0
SPRING = 4.0
LOWER = 0.05
UPPER = 2.0
RADIUS_SQ = 2.0


def beside_cells(field):
    widths = [(0, 0)] * (field.ndim - 3) + [(1, 1)] * 3
    padded = jnp.pad(field, widths)
    return [padded[..., 2:, 1:-1, 1:-1], padded[..., :-2, 1:-1, 1:-1],
            padded[..., 1:-1, 2:, 1:-1], padded[..., 1:-1, :-2, 1:-1],
            padded[..., 1:-1, 1:-1, 2:], padded[..., 1:-1, 1:-1, :-2]]


def forces(index, table):
    parts = []
    for component in range(3):
        total = jnp.zeros(index.shape, jnp.float32)
        for entry in range(table.shape[0]):
            total = total + jnp.where(index == entry, table[entry, component], jnp.float32(0.0))
        parts.append(total)
    return jnp.stack(parts, axis=-4)


def operate(stiffness, diagonal, field):
    total = diagonal * field
    for weight, other in zip(stiffness, beside_cells(field)):
        total = total - weight * other
    return total


def reference(density, support, loads, load_table):
    modulus = E_MIN + density ** 3 * (1.0 - E_MIN)
    stiffness = [(modulus + other) * 0.5 for other in beside_cells(modulus)]
    diagonal = sum(stiffness) + SPRING * support.astype(jnp.float32)
    centre = (UPPER + LOWER) / 2.0
    half = (UPPER - LOWER) / 2.0
    sigma = centre / half
    energy = jnp.zeros(density.shape, jnp.float32)
    moved = []
    for case_index in range(LOADS):
        residual = forces(loads[case_index], load_table)
        search = residual / diagonal / centre
        iterate = search
        factor_old = 1.0 / sigma
        for sweep in range(1, ITERS):
            residual = residual - operate(stiffness, diagonal, search)
            factor_new = 1.0 / (2.0 * sigma - factor_old)
            search = factor_new * factor_old * search + (2.0 * factor_new / half) * residual / diagonal
            iterate = iterate + search
            factor_old = factor_new
        moved.append(iterate)
        for other in beside_cells(iterate):
            energy = energy + 0.5 * jnp.sum((iterate - other) ** 2, axis=0)
    sensitivity = -PENALTY * density ** 2 * (1.0 - E_MIN) * energy
    right = density * sensitivity
    smooth = right
    for sweep in range(FSWEEPS):
        beside = beside_cells(smooth)
        total = beside[0] + beside[1] + beside[2] + beside[3] + beside[4] + beside[5]
        smooth = (right + RADIUS_SQ * total) / (1.0 + 6.0 * RADIUS_SQ)
    return jnp.stack(moved), smooth / density
```

```python
import jax
import jax.numpy as jnp
from jax import lax
from jax.experimental import pallas as pl
from jax.experimental.pallas import tpu as pltpu
from jax.sharding import PartitionSpec as P

ITERS = 3
FSWEEPS = 4

E_MIN = 0.001
PENALTY = 3.0
SPRING = 4.0
LOWER = 0.05
UPPER = 2.0
RADIUS_SQ = 2.0

CENTRE = (UPPER + LOWER) / 2.0
HALF = (UPPER - LOWER) / 2.0
SIGMA = CENTRE / HALF
RHO0 = 1.0 / SIGMA
RHO1 = 1.0 / (2.0 * SIGMA - RHO0)
RHO2 = 1.0 / (2.0 * SIGMA - RHO1)
ALPHA1, B1 = RHO1 * RHO0, 2.0 * RHO1 / HALF
ALPHA2, B2 = RHO2 * RHO1, 2.0 * RHO2 / HALF
G0 = ALPHA1 + B1 * (CENTRE - 1.0)
A0 = 1.0 - B2 * ALPHA1 / B1
A1 = 1.0 + ALPHA2 + B2 / B1 - B2
RATIO = B2 / B1

HALO = 4
EXTRA = 8
PAD = 8


def step_kernel(planes, rows, info, table, valid, loads, support, mid, lo_d, hi_d, lo_i, hi_i, *rest):
    (u_out, e_out, idx_v, sup_v, m_v, k_v, s0_v, s1_v, u_v, in_sem, out_sem) = rest[-11:]
    tiles = rows // 8
    h = info[0]
    vlo, vhi = valid[0], valid[1]
    start = pl.multiple_of(h * info[1], 8)
    wide = planes + 6
    copies = []
    for case in range(2):
        copies.append(pltpu.make_async_copy(
            loads.at[case, :, pl.ds(start, rows), :], idx_v.at[case, pl.ds(3, planes)], in_sem.at[case]))
        copies.append(pltpu.make_async_copy(lo_i.at[pl.ds(3 * case, 3)], idx_v.at[case, pl.ds(0, 3)], in_sem.at[2 + case]))
        copies.append(pltpu.make_async_copy(hi_i.at[pl.ds(3 * case, 3)], idx_v.at[case, pl.ds(planes + 3, 3)], in_sem.at[4 + case]))
    copies.append(pltpu.make_async_copy(support.at[:, pl.ds(start, rows), :], sup_v.at[pl.ds(3, planes)], in_sem.at[6]))
    copies.append(pltpu.make_async_copy(lo_i.at[pl.ds(6, 3)], sup_v.at[pl.ds(0, 3)], in_sem.at[7]))
    copies.append(pltpu.make_async_copy(hi_i.at[pl.ds(6, 3)], sup_v.at[pl.ds(planes + 3, 3)], in_sem.at[8]))
    for copy in copies:
        copy.start()

    zero = jnp.zeros((PAD, 128), jnp.float32)
    for z in range(2):
        def clear(count, ref):
            def body(i, carry):
                ref[i, z, pl.ds(0, PAD), :] = zero
                ref[i, z, pl.ds(PAD + rows, PAD), :] = zero
                return carry
            lax.fori_loop(0, count, body, 0)
        clear(planes + 8, m_v)
        clear(6 * (planes + 6), s0_v)
        clear(6 * (planes + 4), s1_v)
        clear(6 * (planes + 2), u_v)

    def modulus(source, first, count, scale):
        def body(i, carry):
            p, r = i // tiles, pl.multiple_of(i % tiles * 8, 8)
            for z in range(2):
                d = source[p, pl.ds(r, 8), pl.ds(128 * z, 128)]
                m = E_MIN + d * d * d * (1.0 - E_MIN)
                if scale is not None:
                    m = m * scale
                m_v[first + p, z, pl.ds(PAD + r, 8), :] = m
            return carry
        lax.fori_loop(0, count * tiles, body, 0)

    modulus(lo_d, 0, 4, vlo)
    modulus(mid, 4, planes, None)
    modulus(hi_d, planes + 4, 4, vhi)

    lane = lax.broadcasted_iota(jnp.int32, (8, 128), 1)
    first_lane, last_lane = lane == 0, lane == 127

    def above(a):
        r0, r1 = pltpu.roll(a[0], 127, 1), pltpu.roll(a[1], 127, 1)
        return [jnp.where(last_lane, r1, r0), r1]

    def below(a):
        r0, r1 = pltpu.roll(a[0], 1, 1), pltpu.roll(a[1], 1, 1)
        return [r0, jnp.where(first_lane, r0, r1)]

    def get(ref, i, row):
        return [ref[i, z, pl.ds(row, 8), :] for z in range(2)]

    for copy in copies:
        copy.wait()

    def first(i, carry):
        p, r = i // tiles, pl.multiple_of(i % tiles * 8, 8)
        row = PAD + r
        m = get(m_v, p + 1, row)
        zup, zdn = above(m), below(m)
        zup[1] = jnp.where(last_lane, 0.0, zup[1])
        zdn[0] = jnp.where(first_lane, 0.0, zdn[0])
        beside = [get(m_v, p + 2, row), get(m_v, p, row), get(m_v, p + 1, row + 1), get(m_v, p + 1, row - 1), zup, zdn]
        ok = jnp.where(p < 3, vlo, jnp.where(p >= planes + 3, vhi, 1.0))
        scale = []
        for z in range(2):
            face = [(m[z] + b[z]) * 0.5 for b in beside]
            diagonal = face[0] + face[1] + face[2] + face[3] + face[4] + face[5]
            diagonal = diagonal + SPRING * sup_v[p, pl.ds(r, 8), pl.ds(128 * z, 128)].astype(jnp.float32)
            w = ok / (diagonal + (1.0 - ok))
            scale.append(w * (RATIO / CENTRE))
            wb = w * B1
            weight = [f * wb for f in face]
            if z == 1:
                weight[4] = jnp.where(last_lane, 0.0, weight[4])
            else:
                weight[5] = jnp.where(first_lane, 0.0, weight[5])
            for j in range(6):
                k_v[p, j, z, pl.ds(r, 8), :] = weight[j]
        for case in range(2):
            for z in range(2):
                index = idx_v[case, p, pl.ds(r, 8), pl.ds(128 * z, 128)]
                b0, b1, b2 = (index & 1) != 0, (index & 2) != 0, (index & 4) != 0
                for c in range(3):
                    q = [jnp.where(b0, table[2 * j + 1, c], table[2 * j, c]) for j in range(4)]
                    f = jnp.where(b2, jnp.where(b1, q[3], q[2]), jnp.where(b1, q[1], q[0]))
                    s0_v[p * 6 + case * 3 + c, z, pl.ds(row, 8), :] = f * scale[z]
        return carry

    lax.fori_loop(0, wide * tiles, first, 0)

    def stencil(ref, at, row, k):
        c = get(ref, at, row)
        parts = [get(ref, at + 6, row), get(ref, at - 6, row), get(ref, at, row + 1), get(ref, at, row - 1), above(c), below(c)]
        out = []
        for z in range(2):
            t = [k[j][z] * parts[j][z] for j in range(6)]
            out.append(((t[0] + t[1]) + (t[2] + t[3])) + (t[4] + t[5]))
        return c, out

    def second(i, carry):
        p, r = i // tiles, pl.multiple_of(i % tiles * 8, 8)
        row = PAD + r
        k = [[k_v[p + 1, j, z, pl.ds(r, 8), :] for z in range(2)] for j in range(6)]
        for f in range(6):
            c, t = stencil(s0_v, (p + 1) * 6 + f, row, k)
            for z in range(2):
                s1_v[p * 6 + f, z, pl.ds(row, 8), :] = G0 * c[z] + t[z]
        return carry

    lax.fori_loop(0, (planes + 4) * tiles, second, 0)

    def third(i, carry):
        p, r = i // tiles, pl.multiple_of(i % tiles * 8, 8)
        row = PAD + r
        k = [[k_v[p + 2, j, z, pl.ds(r, 8), :] for z in range(2)] for j in range(6)]
        for f in range(6):
            c, t = stencil(s1_v, (p + 1) * 6 + f, row, k)
            base = get(s0_v, (p + 2) * 6 + f, row)
            for z in range(2):
                u_v[p * 6 + f, z, pl.ds(row, 8), :] = (A0 / RATIO) * base[z] + (A1 / RATIO) * c[z] + t[z]
        return carry

    lax.fori_loop(0, (planes + 2) * tiles, third, 0)

    half = rows - EXTRA
    skip = pl.multiple_of(h * EXTRA, 8)
    outs = []
    for z in range(2):
        for p in range(planes):
            for f in range(6):
                outs.append(pltpu.make_async_copy(
                    u_v.at[(p + 1) * 6 + f, z, pl.ds(PAD + skip, half), :],
                    u_out.at[f // 3, f % 3, p, pl.ds(pl.multiple_of(h * half, 8), half), pl.ds(128 * z, 128)],
                    out_sem.at[(z * planes + p) * 6 + f]))
    for copy in outs:
        copy.start()

    def energy(i, carry):
        p, r = i // tiles, pl.multiple_of(i % tiles * 8, 8)
        row = PAD + r
        acc = [jnp.zeros((8, 128), jnp.float32) for _ in range(2)]
        for f in range(6):
            at = (p + 1) * 6 + f
            c = get(u_v, at, row)
            zup, zdn = above(c), below(c)
            zup[1] = jnp.where(last_lane, 0.0, zup[1])
            zdn[0] = jnp.where(first_lane, 0.0, zdn[0])
            for b in (get(u_v, at + 6, row), get(u_v, at - 6, row), get(u_v, at, row + 1), get(u_v, at, row - 1), zup, zdn):
                for z in range(2):
                    d = c[z] - b[z]
                    acc[z] = acc[z] + d * d
        for z in range(2):
            e_out[p, pl.ds(r, 8), pl.ds(128 * z, 128)] = 0.5 * acc[z]
        return carry

    lax.fori_loop(0, planes * tiles, energy, 0)
    for copy in outs:
        copy.wait()


def step(h, gap, valid, table, loads, support, mid, lo_d, hi_d, lo_i, hi_i, u):
    planes, rows, cols = mid.shape
    tiles_rows = rows + 2 * PAD
    f32 = jnp.float32
    any_spec = pl.BlockSpec(memory_space=pl.ANY)
    smem = pl.BlockSpec(memory_space=pltpu.SMEM)
    vmem = pl.BlockSpec(memory_space=pltpu.VMEM)
    full = loads.shape[2]
    args = [jnp.stack([h, gap]).astype(jnp.int32), table, valid, loads, support, mid, lo_d, hi_d, lo_i, hi_i]
    specs = [smem, smem, smem, any_spec, any_spec, vmem, vmem, vmem, any_spec, any_spec]
    aliases = {}
    if u is not None:
        args.append(u)
        specs.append(any_spec)
        aliases = {len(args) - 1: 0}

    def kernel(*refs):
        step_kernel(planes, rows, *refs)

    return pl.pallas_call(
        kernel,
        out_shape=(jax.ShapeDtypeStruct((2, 3, planes, full, cols), f32), jax.ShapeDtypeStruct((planes, rows, cols), f32)),
        in_specs=specs,
        out_specs=(any_spec, vmem),
        input_output_aliases=aliases,
        scratch_shapes=[
            pltpu.VMEM((2, planes + 6, rows, cols), jnp.int32),
            pltpu.VMEM((planes + 6, rows, cols), jnp.int32),
            pltpu.VMEM((planes + 8, 2, tiles_rows, 128), f32),
            pltpu.VMEM((planes + 6, 6, 2, rows, 128), f32),
            pltpu.VMEM((6 * (planes + 6), 2, tiles_rows, 128), f32),
            pltpu.VMEM((6 * (planes + 4), 2, tiles_rows, 128), f32),
            pltpu.VMEM((6 * (planes + 2), 2, tiles_rows, 128), f32),
            pltpu.SemaphoreType.DMA((9,)),
            pltpu.SemaphoreType.DMA((2 * planes * 6,)),
        ],
        compiler_params=pltpu.CompilerParams(vmem_limit_bytes=56 * 1024 * 1024),
        cost_estimate=pl.CostEstimate(flops=40_000_000, bytes_accessed=40_000_000, transcendentals=0),
        name="relax",
    )(*args)


def filter_kernel(planes, rows, info, valid, lo, mid, hi, dens, out, r_v, a_v, b_v):
    tiles = rows // 8
    h = info[0]
    vlo, vhi = valid[0], valid[1]
    half = rows - EXTRA
    zero = jnp.zeros((PAD, 128), jnp.float32)
    lane = lax.broadcasted_iota(jnp.int32, (8, 128), 1)
    first_lane, last_lane = lane == 0, lane == 127

    def clear(i, carry):
        for ref in (r_v, a_v, b_v):
            for z in range(2):
                ref[i, z, pl.ds(0, PAD), :] = zero
                ref[i, z, pl.ds(PAD + rows, PAD), :] = zero
        return carry

    lax.fori_loop(0, planes + 8, clear, 0)

    def fill(source, first, count):
        def body(i, carry):
            p, r = i // tiles, pl.multiple_of(i % tiles * 8, 8)
            for z in range(2):
                r_v[first + p, z, pl.ds(PAD + r, 8), :] = source[p, pl.ds(r, 8), pl.ds(128 * z, 128)]
            return carry

        lax.fori_loop(0, count * tiles, body, 0)

    fill(lo, 0, 4)
    fill(mid, 4, planes)
    fill(hi, planes + 4, 4)

    def smoothed(src, p, row):
        ok = jnp.where(p < 4, vlo, jnp.where(p >= planes + 4, vhi, 1.0))
        c = [src[p, z, pl.ds(row, 8), :] for z in range(2)]
        u0, u1 = pltpu.roll(c[0], 127, 1), pltpu.roll(c[1], 127, 1)
        d0, d1 = pltpu.roll(c[0], 1, 1), pltpu.roll(c[1], 1, 1)
        zs = [
            jnp.where(last_lane, u1, u0) + jnp.where(first_lane, 0.0, d0),
            jnp.where(last_lane, 0.0, u1) + jnp.where(first_lane, d0, d1),
        ]
        new = []
        for z in range(2):
            total = (src[p + 1, z, pl.ds(row, 8), :] + src[p - 1, z, pl.ds(row, 8), :]) + (
                src[p, z, pl.ds(row + 1, 8), :] + src[p, z, pl.ds(row - 1, 8), :]) + zs[z]
            scale = ok * (1.0 / (1.0 + 6.0 * RADIUS_SQ))
            new.append((r_v[p, z, pl.ds(row, 8), :] + RADIUS_SQ * total) * scale)
        return new

    def sweep(src, dst, low, high):
        def body(i, carry):
            p, row = low + i // tiles, pl.multiple_of(PAD + i % tiles * 8, 8)
            new = smoothed(src, p, row)
            for z in range(2):
                dst[p, z, pl.ds(row, 8), :] = new[z]
            return carry

        lax.fori_loop(0, (high - low) * tiles, body, 0)

    sweep(r_v, a_v, 1, planes + 7)
    sweep(a_v, b_v, 2, planes + 6)
    sweep(b_v, a_v, 3, planes + 5)

    skip = h * EXTRA

    def last(i, carry):
        p, r = i // (half // 8), pl.multiple_of(i % (half // 8) * 8, 8)
        new = smoothed(a_v, p + 4, pl.multiple_of(PAD + r + skip, 8))
        for z in range(2):
            out[p, pl.ds(r, 8), pl.ds(128 * z, 128)] = new[z] / dens[p, pl.ds(r, 8), pl.ds(128 * z, 128)]
        return carry

    lax.fori_loop(0, planes * (half // 8), last, 0)


def smooth(h, gap, valid, lo, mid, hi, dens):
    planes, rows, cols = mid.shape
    f32 = jnp.float32
    smem = pl.BlockSpec(memory_space=pltpu.SMEM)
    vmem = pl.BlockSpec(memory_space=pltpu.VMEM)

    def kernel(*refs):
        filter_kernel(planes, rows, *refs)

    return pl.pallas_call(
        kernel,
        out_shape=jax.ShapeDtypeStruct(dens.shape, f32),
        in_specs=[smem, smem] + [vmem] * 4,
        out_specs=vmem,
        scratch_shapes=[pltpu.VMEM((planes + 8, 2, rows + 2 * PAD, 128), f32)] * 3,
        compiler_params=pltpu.CompilerParams(vmem_limit_bytes=32 * 1024 * 1024),
        cost_estimate=pl.CostEstimate(flops=5_000_000, bytes_accessed=5_000_000, transcendentals=0),
        name="smooth",
    )(jnp.stack([h, gap]).astype(jnp.int32), valid, lo, mid, hi, dens)


def local(density, support, loads, load_table):
    planes, half, cols = density.shape
    full = loads.shape[2]
    rows = half + EXTRA
    gap = full - rows
    mine = lax.axis_index("case")
    count = lax.axis_size("slab")
    at = lax.axis_index("slab")
    valid = jnp.stack([at > 0, at < count - 1]).astype(jnp.float32)
    rise = [(i, i + 1) for i in range(count - 1)]
    fall = [(i + 1, i) for i in range(count - 1)]
    swap = [(0, 1), (1, 0)]

    partner = lax.ppermute(density, "case", swap)

    def window(h):
        start = h * gap
        own = lax.dynamic_slice_in_dim(loads, start, rows, axis=2)
        sup = lax.dynamic_slice_in_dim(support, start, rows, axis=1)

        def pack(a, b):
            return jnp.concatenate([own[0, a:b], own[1, a:b], sup[a:b]], axis=0)

        lo_i = lax.ppermute(pack(planes - 3, planes), "slab", rise)
        hi_i = lax.ppermute(pack(0, 3), "slab", fall)
        return lo_i, hi_i

    def densities(h, main, other):
        low = jnp.concatenate([main, other[:, :EXTRA]], axis=1)
        high = jnp.concatenate([other[:, half - EXTRA:], main], axis=1)
        mid = jnp.where(h == 0, low, high)
        lo_d = lax.ppermute(mid[planes - 4:], "slab", rise)
        hi_d = lax.ppermute(mid[:4], "slab", fall)
        return mid, lo_d, hi_d

    ints_a = window(1 - mine)
    dens_a = densities(1 - mine, partner, density)
    ints_b = window(mine)
    dens_b = densities(mine, density, partner)
    u, e_a = step(1 - mine, gap, valid, load_table, loads, support, *dens_a, *ints_a, None)
    received = lax.ppermute(e_a, "case", swap)
    u, e_b = step(mine, gap, valid, load_table, loads, support, *dens_b, *ints_b, u)
    mid = dens_b[0]
    right = (-PENALTY * (1.0 - E_MIN)) * (mid * mid * mid) * (e_b + received)
    lo_r = lax.ppermute(right[planes - 4:], "slab", rise)
    hi_r = lax.ppermute(right[:4], "slab", fall)
    filtered = smooth(mine, gap, valid, lo_r, right, hi_r, density)
    return u, filtered


def solution(mesh):
    return jax.shard_map(
        local,
        mesh=mesh,
        in_specs=(
            P("slab", "case", None),
            P("slab", None, None),
            P("case", "slab", None, None),
            P(),
        ),
        out_specs=(P("case", None, "slab", None, None), P("slab", "case", None)),
        check_vma=False,
    )
```

```python
import jax
import jax.numpy as jnp
from jax import lax
from jax.experimental import pallas as pl
from jax.experimental.pallas import tpu as pltpu
from jax.sharding import PartitionSpec as P

ITERS = 3
FSWEEPS = 4

E_MIN = 0.001
PENALTY = 3.0
SPRING = 4.0
LOWER = 0.05
UPPER = 2.0
RADIUS_SQ = 2.0

CENTRE = (UPPER + LOWER) / 2.0
HALF = (UPPER - LOWER) / 2.0
SIGMA = CENTRE / HALF
RHO0 = 1.0 / SIGMA
RHO1 = 1.0 / (2.0 * SIGMA - RHO0)
RHO2 = 1.0 / (2.0 * SIGMA - RHO1)
ALPHA1, B1 = RHO1 * RHO0, 2.0 * RHO1 / HALF
ALPHA2, B2 = RHO2 * RHO1, 2.0 * RHO2 / HALF
G0 = ALPHA1 + B1 * (CENTRE - 1.0)
A0 = 1.0 - B2 * ALPHA1 / B1
A1 = 1.0 + ALPHA2 + B2 / B1 - B2
RATIO = B2 / B1

UM = 17
U0 = 17
U1 = 17
U2 = 17
UE = 17
UF = 8
HALO = 4
EXTRA = 8
PAD = 8


def sweep_rows(count, tiles, body, unroll):
    def outer(p, carry):
        def inner(j, c):
            body(p, pl.multiple_of(j * 8, 8))
            return c
        return lax.fori_loop(0, tiles, inner, carry, unroll=unroll)
    lax.fori_loop(0, count, outer, 0)


def step_kernel(planes, rows, info, table, valid, loads, support, mid, lo_d, hi_d, lo_i, hi_i, *rest):
    (u_out, e_out, idx_v, sup_v, m_v, k_v, s0_v, s1_v, u_v, in_sem, out_sem) = rest[-11:]
    tiles = rows // 8
    h = info[0]
    vlo, vhi = valid[0], valid[1]
    start = pl.multiple_of(h * info[1], 8)
    wide = planes + 6
    copies = []
    for case in range(2):
        copies.append(pltpu.make_async_copy(
            loads.at[case, :, pl.ds(start, rows), :], idx_v.at[case, pl.ds(3, planes)], in_sem.at[case]))
        copies.append(pltpu.make_async_copy(lo_i.at[pl.ds(3 * case, 3)], idx_v.at[case, pl.ds(0, 3)], in_sem.at[2 + case]))
        copies.append(pltpu.make_async_copy(hi_i.at[pl.ds(3 * case, 3)], idx_v.at[case, pl.ds(planes + 3, 3)], in_sem.at[4 + case]))
    copies.append(pltpu.make_async_copy(support.at[:, pl.ds(start, rows), :], sup_v.at[pl.ds(3, planes)], in_sem.at[6]))
    copies.append(pltpu.make_async_copy(lo_i.at[pl.ds(6, 3)], sup_v.at[pl.ds(0, 3)], in_sem.at[7]))
    copies.append(pltpu.make_async_copy(hi_i.at[pl.ds(6, 3)], sup_v.at[pl.ds(planes + 3, 3)], in_sem.at[8]))
    for copy in copies:
        copy.start()

    zero = jnp.zeros((PAD, 128), jnp.float32)
    for z in range(2):
        def clear(count, ref):
            def body(i, carry):
                ref[i, z, pl.ds(0, PAD), :] = zero
                ref[i, z, pl.ds(PAD + rows, PAD), :] = zero
                return carry
            lax.fori_loop(0, count, body, 0)
        clear(planes + 8, m_v)
        clear(6 * (planes + 6), s0_v)
        clear(6 * (planes + 4), s1_v)
        clear(6 * (planes + 2), u_v)

    def modulus(source, first, count, scale):
        def body(p, r):
            for z in range(2):
                d = source[p, pl.ds(r, 8), pl.ds(128 * z, 128)]
                m = E_MIN + d * d * d * (1.0 - E_MIN)
                if scale is not None:
                    m = m * scale
                m_v[first + p, z, pl.ds(PAD + r, 8), :] = m
        sweep_rows(count, tiles, body, UM)

    modulus(lo_d, 0, 4, vlo)
    modulus(mid, 4, planes, None)
    modulus(hi_d, planes + 4, 4, vhi)

    lane = lax.broadcasted_iota(jnp.int32, (8, 128), 1)
    first_lane, last_lane = lane == 0, lane == 127

    def above(a):
        r0, r1 = pltpu.roll(a[0], 127, 1), pltpu.roll(a[1], 127, 1)
        return [jnp.where(last_lane, r1, r0), r1]

    def below(a):
        r0, r1 = pltpu.roll(a[0], 1, 1), pltpu.roll(a[1], 1, 1)
        return [r0, jnp.where(first_lane, r0, r1)]

    def get(ref, i, row):
        return [ref[i, z, pl.ds(row, 8), :] for z in range(2)]

    for copy in copies:
        copy.wait()

    def first(p, r):
        row = PAD + r
        m = get(m_v, p + 1, row)
        zup, zdn = above(m), below(m)
        zup[1] = jnp.where(last_lane, 0.0, zup[1])
        zdn[0] = jnp.where(first_lane, 0.0, zdn[0])
        beside = [get(m_v, p + 2, row), get(m_v, p, row), get(m_v, p + 1, row + 1), get(m_v, p + 1, row - 1), zup, zdn]
        ok = jnp.where(p < 3, vlo, jnp.where(p >= planes + 3, vhi, 1.0))
        scale = []
        for z in range(2):
            face = [(m[z] + b[z]) * 0.5 for b in beside]
            diagonal = face[0] + face[1] + face[2] + face[3] + face[4] + face[5]
            diagonal = diagonal + SPRING * sup_v[p, pl.ds(r, 8), pl.ds(128 * z, 128)].astype(jnp.float32)
            w = ok / (diagonal + (1.0 - ok))
            scale.append(w * (RATIO / CENTRE))
            wb = w * B1
            weight = [f * wb for f in face]
            if z == 1:
                weight[4] = jnp.where(last_lane, 0.0, weight[4])
            else:
                weight[5] = jnp.where(first_lane, 0.0, weight[5])
            for j in range(6):
                k_v[p, j, z, pl.ds(r, 8), :] = weight[j]
        for case in range(2):
            for z in range(2):
                index = idx_v[case, p, pl.ds(r, 8), pl.ds(128 * z, 128)]
                b0, b1, b2 = (index & 1) != 0, (index & 2) != 0, (index & 4) != 0
                for c in range(3):
                    q = [jnp.where(b0, table[2 * j + 1, c], table[2 * j, c]) for j in range(4)]
                    f = jnp.where(b2, jnp.where(b1, q[3], q[2]), jnp.where(b1, q[1], q[0]))
                    s0_v[p * 6 + case * 3 + c, z, pl.ds(row, 8), :] = f * scale[z]

    sweep_rows(wide, tiles, first, U0)

    def stencil(ref, at, row, k):
        c = get(ref, at, row)
        parts = [get(ref, at + 6, row), get(ref, at - 6, row), get(ref, at, row + 1), get(ref, at, row - 1), above(c), below(c)]
        out = []
        for z in range(2):
            t = [k[j][z] * parts[j][z] for j in range(6)]
            out.append(((t[0] + t[1]) + (t[2] + t[3])) + (t[4] + t[5]))
        return c, out

    def second(p, r):
        row = PAD + r
        k = [[k_v[p + 1, j, z, pl.ds(r, 8), :] for z in range(2)] for j in range(6)]
        for f in range(6):
            c, t = stencil(s0_v, (p + 1) * 6 + f, row, k)
            for z in range(2):
                s1_v[p * 6 + f, z, pl.ds(row, 8), :] = G0 * c[z] + t[z]

    sweep_rows((planes + 4), tiles, second, U1)

    def third(p, r):
        row = PAD + r
        k = [[k_v[p + 2, j, z, pl.ds(r, 8), :] for z in range(2)] for j in range(6)]
        for f in range(6):
            c, t = stencil(s1_v, (p + 1) * 6 + f, row, k)
            base = get(s0_v, (p + 2) * 6 + f, row)
            for z in range(2):
                u_v[p * 6 + f, z, pl.ds(row, 8), :] = (A0 / RATIO) * base[z] + (A1 / RATIO) * c[z] + t[z]

    sweep_rows((planes + 2), tiles, third, U2)

    half = rows - EXTRA
    skip = pl.multiple_of(h * EXTRA, 8)
    outs = []
    for z in range(2):
        for p in range(planes):
            for f in range(6):
                outs.append(pltpu.make_async_copy(
                    u_v.at[(p + 1) * 6 + f, z, pl.ds(PAD + skip, half), :],
                    u_out.at[f // 3, f % 3, p, pl.ds(pl.multiple_of(h * half, 8), half), pl.ds(128 * z, 128)],
                    out_sem.at[(z * planes + p) * 6 + f]))
    for copy in outs:
        copy.start()

    def energy(p, r):
        row = PAD + r
        acc = [jnp.zeros((8, 128), jnp.float32) for _ in range(2)]
        for f in range(6):
            at = (p + 1) * 6 + f
            c = get(u_v, at, row)
            zup, zdn = above(c), below(c)
            zup[1] = jnp.where(last_lane, 0.0, zup[1])
            zdn[0] = jnp.where(first_lane, 0.0, zdn[0])
            for b in (get(u_v, at + 6, row), get(u_v, at - 6, row), get(u_v, at, row + 1), get(u_v, at, row - 1), zup, zdn):
                for z in range(2):
                    d = c[z] - b[z]
                    acc[z] = acc[z] + d * d
        for z in range(2):
            e_out[p, pl.ds(r, 8), pl.ds(128 * z, 128)] = 0.5 * acc[z]

    sweep_rows(planes, tiles, energy, UE)
    for copy in outs:
        copy.wait()


def step(h, gap, valid, table, loads, support, mid, lo_d, hi_d, lo_i, hi_i, u):
    planes, rows, cols = mid.shape
    tiles_rows = rows + 2 * PAD
    f32 = jnp.float32
    any_spec = pl.BlockSpec(memory_space=pl.ANY)
    smem = pl.BlockSpec(memory_space=pltpu.SMEM)
    vmem = pl.BlockSpec(memory_space=pltpu.VMEM)
    full = loads.shape[2]
    args = [jnp.stack([h, gap]).astype(jnp.int32), table, valid, loads, support, mid, lo_d, hi_d, lo_i, hi_i]
    specs = [smem, smem, smem, any_spec, any_spec, vmem, vmem, vmem, any_spec, any_spec]
    aliases = {}
    if u is not None:
        args.append(u)
        specs.append(any_spec)
        aliases = {len(args) - 1: 0}

    def kernel(*refs):
        step_kernel(planes, rows, *refs)

    return pl.pallas_call(
        kernel,
        out_shape=(jax.ShapeDtypeStruct((2, 3, planes, full, cols), f32), jax.ShapeDtypeStruct((planes, rows, cols), f32)),
        in_specs=specs,
        out_specs=(any_spec, vmem),
        input_output_aliases=aliases,
        scratch_shapes=[
            pltpu.VMEM((2, planes + 6, rows, cols), jnp.int32),
            pltpu.VMEM((planes + 6, rows, cols), jnp.int32),
            pltpu.VMEM((planes + 8, 2, tiles_rows, 128), f32),
            pltpu.VMEM((planes + 6, 6, 2, rows, 128), f32),
            pltpu.VMEM((6 * (planes + 6), 2, tiles_rows, 128), f32),
            pltpu.VMEM((6 * (planes + 4), 2, tiles_rows, 128), f32),
            pltpu.VMEM((6 * (planes + 2), 2, tiles_rows, 128), f32),
            pltpu.SemaphoreType.DMA((9,)),
            pltpu.SemaphoreType.DMA((2 * planes * 6,)),
        ],
        compiler_params=pltpu.CompilerParams(vmem_limit_bytes=56 * 1024 * 1024),
        cost_estimate=pl.CostEstimate(flops=40_000_000, bytes_accessed=40_000_000, transcendentals=0),
        name="relax",
    )(*args)


def filter_kernel(planes, rows, info, valid, lo, mid, hi, dens, out, r_v, a_v, b_v):
    tiles = rows // 8
    h = info[0]
    vlo, vhi = valid[0], valid[1]
    half = rows - EXTRA
    zero = jnp.zeros((PAD, 128), jnp.float32)
    lane = lax.broadcasted_iota(jnp.int32, (8, 128), 1)
    first_lane, last_lane = lane == 0, lane == 127

    def clear(i, carry):
        for ref in (r_v, a_v, b_v):
            for z in range(2):
                ref[i, z, pl.ds(0, PAD), :] = zero
                ref[i, z, pl.ds(PAD + rows, PAD), :] = zero
        return carry

    lax.fori_loop(0, planes + 8, clear, 0)

    def fill(source, first, count):
        def body(p, r):
            for z in range(2):
                r_v[first + p, z, pl.ds(PAD + r, 8), :] = source[p, pl.ds(r, 8), pl.ds(128 * z, 128)]

        sweep_rows(count, tiles, body, UM)

    fill(lo, 0, 4)
    fill(mid, 4, planes)
    fill(hi, planes + 4, 4)

    def smoothed(src, p, row):
        ok = jnp.where(p < 4, vlo, jnp.where(p >= planes + 4, vhi, 1.0))
        c = [src[p, z, pl.ds(row, 8), :] for z in range(2)]
        u0, u1 = pltpu.roll(c[0], 127, 1), pltpu.roll(c[1], 127, 1)
        d0, d1 = pltpu.roll(c[0], 1, 1), pltpu.roll(c[1], 1, 1)
        zs = [
            jnp.where(last_lane, u1, u0) + jnp.where(first_lane, 0.0, d0),
            jnp.where(last_lane, 0.0, u1) + jnp.where(first_lane, d0, d1),
        ]
        new = []
        for z in range(2):
            total = (src[p + 1, z, pl.ds(row, 8), :] + src[p - 1, z, pl.ds(row, 8), :]) + (
                src[p, z, pl.ds(row + 1, 8), :] + src[p, z, pl.ds(row - 1, 8), :]) + zs[z]
            scale = ok * (1.0 / (1.0 + 6.0 * RADIUS_SQ))
            new.append((r_v[p, z, pl.ds(row, 8), :] + RADIUS_SQ * total) * scale)
        return new

    def sweep(src, dst, low, high):
        def body(p, r):
            p, row = low + p, PAD + r
            new = smoothed(src, p, row)
            for z in range(2):
                dst[p, z, pl.ds(row, 8), :] = new[z]

        sweep_rows((high - low), tiles, body, UF)

    sweep(r_v, a_v, 1, planes + 7)
    sweep(a_v, b_v, 2, planes + 6)
    sweep(b_v, a_v, 3, planes + 5)

    skip = h * EXTRA

    def last(p, r):
        new = smoothed(a_v, p + 4, pl.multiple_of(PAD + r + skip, 8))
        for z in range(2):
            out[p, pl.ds(r, 8), pl.ds(128 * z, 128)] = new[z] / dens[p, pl.ds(r, 8), pl.ds(128 * z, 128)]

    sweep_rows(planes, half // 8, last, UF)


def smooth(h, gap, valid, lo, mid, hi, dens):
    planes, rows, cols = mid.shape
    f32 = jnp.float32
    smem = pl.BlockSpec(memory_space=pltpu.SMEM)
    vmem = pl.BlockSpec(memory_space=pltpu.VMEM)

    def kernel(*refs):
        filter_kernel(planes, rows, *refs)

    return pl.pallas_call(
        kernel,
        out_shape=jax.ShapeDtypeStruct(dens.shape, f32),
        in_specs=[smem, smem] + [vmem] * 4,
        out_specs=vmem,
        scratch_shapes=[pltpu.VMEM((planes + 8, 2, rows + 2 * PAD, 128), f32)] * 3,
        compiler_params=pltpu.CompilerParams(vmem_limit_bytes=32 * 1024 * 1024),
        cost_estimate=pl.CostEstimate(flops=5_000_000, bytes_accessed=5_000_000, transcendentals=0),
        name="smooth",
    )(jnp.stack([h, gap]).astype(jnp.int32), valid, lo, mid, hi, dens)


def local(density, support, loads, load_table):
    planes, half, cols = density.shape
    full = loads.shape[2]
    rows = half + EXTRA
    gap = full - rows
    mine = lax.axis_index("case")
    count = lax.axis_size("slab")
    at = lax.axis_index("slab")
    valid = jnp.stack([at > 0, at < count - 1]).astype(jnp.float32)
    rise = [(i, i + 1) for i in range(count - 1)]
    fall = [(i + 1, i) for i in range(count - 1)]
    swap = [(0, 1), (1, 0)]

    partner = lax.ppermute(density, "case", swap)

    def window(h):
        start = h * gap
        own = lax.dynamic_slice_in_dim(loads, start, rows, axis=2)
        sup = lax.dynamic_slice_in_dim(support, start, rows, axis=1)

        def pack(a, b):
            return jnp.concatenate([own[0, a:b], own[1, a:b], sup[a:b]], axis=0)

        lo_i = lax.ppermute(pack(planes - 3, planes), "slab", rise)
        hi_i = lax.ppermute(pack(0, 3), "slab", fall)
        return lo_i, hi_i

    def densities(h, main, other):
        low = jnp.concatenate([main, other[:, :EXTRA]], axis=1)
        high = jnp.concatenate([other[:, half - EXTRA:], main], axis=1)
        mid = jnp.where(h == 0, low, high)
        lo_d = lax.ppermute(mid[planes - 4:], "slab", rise)
        hi_d = lax.ppermute(mid[:4], "slab", fall)
        return mid, lo_d, hi_d

    ints_a = window(1 - mine)
    dens_a = densities(1 - mine, partner, density)
    ints_b = window(mine)
    dens_b = densities(mine, density, partner)
    u, e_a = step(1 - mine, gap, valid, load_table, loads, support, *dens_a, *ints_a, None)
    received = lax.ppermute(e_a, "case", swap)
    u, e_b = step(mine, gap, valid, load_table, loads, support, *dens_b, *ints_b, u)
    mid = dens_b[0]
    right = (-PENALTY * (1.0 - E_MIN)) * (mid * mid * mid) * (e_b + received)
    lo_r = lax.ppermute(right[planes - 4:], "slab", rise)
    hi_r = lax.ppermute(right[:4], "slab", fall)
    filtered = smooth(mine, gap, valid, lo_r, right, hi_r, density)
    return u, filtered


def solution(mesh):
    return jax.shard_map(
        local,
        mesh=mesh,
        in_specs=(
            P("slab", "case", None),
            P("slab", None, None),
            P("case", "slab", None, None),
            P(),
        ),
        out_specs=(P("case", None, "slab", None, None), P("slab", "case", None)),
        check_vma=False,
    )
```

```python
import jax
import jax.numpy as jnp
from jax import lax
from jax.experimental import pallas as pl
from jax.experimental.pallas import tpu as pltpu
from jax.sharding import PartitionSpec as P

ITERS = 3
FSWEEPS = 4

E_MIN = 0.001
PENALTY = 3.0
SPRING = 4.0
LOWER = 0.05
UPPER = 2.0
RADIUS_SQ = 2.0

CENTRE = (UPPER + LOWER) / 2.0
HALF = (UPPER - LOWER) / 2.0
SIGMA = CENTRE / HALF
RHO0 = 1.0 / SIGMA
RHO1 = 1.0 / (2.0 * SIGMA - RHO0)
RHO2 = 1.0 / (2.0 * SIGMA - RHO1)
ALPHA1, B1 = RHO1 * RHO0, 2.0 * RHO1 / HALF
ALPHA2, B2 = RHO2 * RHO1, 2.0 * RHO2 / HALF
G0 = ALPHA1 + B1 * (CENTRE - 1.0)
A0 = 1.0 - B2 * ALPHA1 / B1
A1 = 1.0 + ALPHA2 + B2 / B1 - B2
RATIO = B2 / B1

UM = 17
U0 = 17
U1 = 17
U2 = 17
UE = 17
UF = 8
HALO = 4
EXTRA = 8
PAD = 8


def sweep_rows(count, tiles, body, unroll):
    def outer(p, carry):
        def inner(j, c):
            body(p, pl.multiple_of(j * 8, 8))
            return c
        return lax.fori_loop(0, tiles, inner, carry, unroll=unroll)
    lax.fori_loop(0, count, outer, 0)


def step_kernel(planes, rows, info, table, valid, loads, support, lo_d, mid, hi_d, lo_x, mid_x, hi_x, lo_i, hi_i, *rest):
    (u_out, e_out, d_v, idx_v, sup_v, m_v, k_v, s0_v, s1_v, u_v, in_sem, out_sem) = rest[-12:]
    tiles = rows // 8
    h = info[0]
    vlo, vhi = valid[0], valid[1]
    start = pl.multiple_of(h * info[1], 8)
    wide = planes + 6
    half = rows - EXTRA
    skip = pl.multiple_of(h * EXTRA, 8)
    copies = []
    for j, (own, other, first_p, count_p) in enumerate((
            (lo_d, lo_x, 0, 4), (mid, mid_x, 4, planes), (hi_d, hi_x, planes + 4, 4))):
        copies.append(pltpu.make_async_copy(
            own, d_v.at[pl.ds(first_p, count_p), pl.ds(skip, half), :], in_sem.at[9 + 2 * j]))
        copies.append(pltpu.make_async_copy(
            other.at[:, pl.ds(pl.multiple_of(h * (half - EXTRA), 8), EXTRA), :],
            d_v.at[pl.ds(first_p, count_p), pl.ds(pl.multiple_of((1 - h) * half, 8), EXTRA), :], in_sem.at[10 + 2 * j]))
    densities = len(copies)
    for case in range(2):
        copies.append(pltpu.make_async_copy(
            loads.at[case, :, pl.ds(start, rows), :], idx_v.at[case, pl.ds(3, planes)], in_sem.at[case]))
        copies.append(pltpu.make_async_copy(lo_i.at[pl.ds(3 * case, 3)], idx_v.at[case, pl.ds(0, 3)], in_sem.at[2 + case]))
        copies.append(pltpu.make_async_copy(hi_i.at[pl.ds(3 * case, 3)], idx_v.at[case, pl.ds(planes + 3, 3)], in_sem.at[4 + case]))
    copies.append(pltpu.make_async_copy(support.at[:, pl.ds(start, rows), :], sup_v.at[pl.ds(3, planes)], in_sem.at[6]))
    copies.append(pltpu.make_async_copy(lo_i.at[pl.ds(6, 3)], sup_v.at[pl.ds(0, 3)], in_sem.at[7]))
    copies.append(pltpu.make_async_copy(hi_i.at[pl.ds(6, 3)], sup_v.at[pl.ds(planes + 3, 3)], in_sem.at[8]))
    for copy in copies:
        copy.start()

    zero = jnp.zeros((PAD, 128), jnp.float32)
    for z in range(2):
        def clear(count, ref):
            def body(i, carry):
                ref[i, z, pl.ds(0, PAD), :] = zero
                ref[i, z, pl.ds(PAD + rows, PAD), :] = zero
                return carry
            lax.fori_loop(0, count, body, 0)
        clear(planes + 8, m_v)
        clear(6 * (planes + 6), s0_v)
        clear(6 * (planes + 4), s1_v)
        clear(6 * (planes + 2), u_v)

    for copy in copies[:densities]:
        copy.wait()

    def modulus(p, r):
        ok = jnp.where(p < 4, vlo, jnp.where(p >= planes + 4, vhi, 1.0))
        for z in range(2):
            d = d_v[p, pl.ds(r, 8), pl.ds(128 * z, 128)]
            m_v[p, z, pl.ds(PAD + r, 8), :] = (E_MIN + d * d * d * (1.0 - E_MIN)) * ok

    sweep_rows(planes + 8, tiles, modulus, UM)

    lane = lax.broadcasted_iota(jnp.int32, (8, 128), 1)
    first_lane, last_lane = lane == 0, lane == 127

    def above(a):
        r0, r1 = pltpu.roll(a[0], 127, 1), pltpu.roll(a[1], 127, 1)
        return [jnp.where(last_lane, r1, r0), r1]

    def below(a):
        r0, r1 = pltpu.roll(a[0], 1, 1), pltpu.roll(a[1], 1, 1)
        return [r0, jnp.where(first_lane, r0, r1)]

    def get(ref, i, row):
        return [ref[i, z, pl.ds(row, 8), :] for z in range(2)]

    for copy in copies[densities:]:
        copy.wait()

    def first(p, r):
        row = PAD + r
        m = get(m_v, p + 1, row)
        zup, zdn = above(m), below(m)
        zup[1] = jnp.where(last_lane, 0.0, zup[1])
        zdn[0] = jnp.where(first_lane, 0.0, zdn[0])
        beside = [get(m_v, p + 2, row), get(m_v, p, row), get(m_v, p + 1, row + 1), get(m_v, p + 1, row - 1), zup, zdn]
        ok = jnp.where(p < 3, vlo, jnp.where(p >= planes + 3, vhi, 1.0))
        scale = []
        for z in range(2):
            face = [(m[z] + b[z]) * 0.5 for b in beside]
            diagonal = face[0] + face[1] + face[2] + face[3] + face[4] + face[5]
            diagonal = diagonal + SPRING * sup_v[p, pl.ds(r, 8), pl.ds(128 * z, 128)].astype(jnp.float32)
            w = ok / (diagonal + (1.0 - ok))
            scale.append(w * (RATIO / CENTRE))
            wb = w * B1
            weight = [f * wb for f in face]
            if z == 1:
                weight[4] = jnp.where(last_lane, 0.0, weight[4])
            else:
                weight[5] = jnp.where(first_lane, 0.0, weight[5])
            for j in range(6):
                k_v[p, j, z, pl.ds(r, 8), :] = weight[j]
        for case in range(2):
            for z in range(2):
                index = idx_v[case, p, pl.ds(r, 8), pl.ds(128 * z, 128)]
                b0, b1, b2 = (index & 1) != 0, (index & 2) != 0, (index & 4) != 0
                for c in range(3):
                    q = [jnp.where(b0, table[2 * j + 1, c], table[2 * j, c]) for j in range(4)]
                    f = jnp.where(b2, jnp.where(b1, q[3], q[2]), jnp.where(b1, q[1], q[0]))
                    s0_v[p * 6 + case * 3 + c, z, pl.ds(row, 8), :] = f * scale[z]

    sweep_rows(wide, tiles, first, U0)

    def stencil(ref, at, row, k):
        c = get(ref, at, row)
        parts = [get(ref, at + 6, row), get(ref, at - 6, row), get(ref, at, row + 1), get(ref, at, row - 1), above(c), below(c)]
        out = []
        for z in range(2):
            t = [k[j][z] * parts[j][z] for j in range(6)]
            out.append(((t[0] + t[1]) + (t[2] + t[3])) + (t[4] + t[5]))
        return c, out

    def second(p, r):
        row = PAD + r
        k = [[k_v[p + 1, j, z, pl.ds(r, 8), :] for z in range(2)] for j in range(6)]
        for f in range(6):
            c, t = stencil(s0_v, (p + 1) * 6 + f, row, k)
            for z in range(2):
                s1_v[p * 6 + f, z, pl.ds(row, 8), :] = G0 * c[z] + t[z]

    sweep_rows((planes + 4), tiles, second, U1)

    def third(p, r):
        row = PAD + r
        k = [[k_v[p + 2, j, z, pl.ds(r, 8), :] for z in range(2)] for j in range(6)]
        for f in range(6):
            c, t = stencil(s1_v, (p + 1) * 6 + f, row, k)
            base = get(s0_v, (p + 2) * 6 + f, row)
            for z in range(2):
                u_v[p * 6 + f, z, pl.ds(row, 8), :] = (A0 / RATIO) * base[z] + (A1 / RATIO) * c[z] + t[z]

    sweep_rows((planes + 2), tiles, third, U2)

    outs = []
    for z in range(2):
        for p in range(planes):
            for f in range(6):
                outs.append(pltpu.make_async_copy(
                    u_v.at[(p + 1) * 6 + f, z, pl.ds(PAD + skip, half), :],
                    u_out.at[f // 3, f % 3, p, pl.ds(pl.multiple_of(h * half, 8), half), pl.ds(128 * z, 128)],
                    out_sem.at[(z * planes + p) * 6 + f]))
    for copy in outs:
        copy.start()

    def energy(p, r):
        row = PAD + r
        acc = [jnp.zeros((8, 128), jnp.float32) for _ in range(2)]
        for f in range(6):
            at = (p + 1) * 6 + f
            c = get(u_v, at, row)
            zup, zdn = above(c), below(c)
            zup[1] = jnp.where(last_lane, 0.0, zup[1])
            zdn[0] = jnp.where(first_lane, 0.0, zdn[0])
            for b in (get(u_v, at + 6, row), get(u_v, at - 6, row), get(u_v, at, row + 1), get(u_v, at, row - 1), zup, zdn):
                for z in range(2):
                    d = c[z] - b[z]
                    acc[z] = acc[z] + d * d
        for z in range(2):
            e_out[p, pl.ds(r, 8), pl.ds(128 * z, 128)] = 0.5 * acc[z]

    sweep_rows(planes, tiles, energy, UE)
    for copy in outs:
        copy.wait()


def step(h, gap, valid, table, loads, support, main, other, ints, u):
    planes, half, cols = main[1].shape
    rows = half + EXTRA
    tiles_rows = rows + 2 * PAD
    f32 = jnp.float32
    any_spec = pl.BlockSpec(memory_space=pl.ANY)
    smem = pl.BlockSpec(memory_space=pltpu.SMEM)
    vmem = pl.BlockSpec(memory_space=pltpu.VMEM)
    full = loads.shape[2]
    args = [jnp.stack([h, gap]).astype(jnp.int32), table, valid, loads, support, *main, *other, *ints]
    specs = [smem, smem, smem] + [any_spec] * 10
    aliases = {}
    if u is not None:
        args.append(u)
        specs.append(any_spec)
        aliases = {len(args) - 1: 0}

    def kernel(*refs):
        step_kernel(planes, rows, *refs)

    return pl.pallas_call(
        kernel,
        out_shape=(jax.ShapeDtypeStruct((2, 3, planes, full, cols), f32), jax.ShapeDtypeStruct((planes, rows, cols), f32)),
        in_specs=specs,
        out_specs=(any_spec, vmem),
        input_output_aliases=aliases,
        scratch_shapes=[
            pltpu.VMEM((planes + 8, rows, cols), f32),
            pltpu.VMEM((2, planes + 6, rows, cols), jnp.int32),
            pltpu.VMEM((planes + 6, rows, cols), jnp.int32),
            pltpu.VMEM((planes + 8, 2, tiles_rows, 128), f32),
            pltpu.VMEM((planes + 6, 6, 2, rows, 128), f32),
            pltpu.VMEM((6 * (planes + 6), 2, tiles_rows, 128), f32),
            pltpu.VMEM((6 * (planes + 4), 2, tiles_rows, 128), f32),
            pltpu.VMEM((6 * (planes + 2), 2, tiles_rows, 128), f32),
            pltpu.SemaphoreType.DMA((15,)),
            pltpu.SemaphoreType.DMA((2 * planes * 6,)),
        ],
        compiler_params=pltpu.CompilerParams(vmem_limit_bytes=56 * 1024 * 1024),
        cost_estimate=pl.CostEstimate(flops=40_000_000, bytes_accessed=40_000_000, transcendentals=0),
        name="relax",
    )(*args)


def filter_kernel(planes, rows, info, valid, lo, mid, hi, dens, out, r_v, a_v, b_v):
    tiles = rows // 8
    h = info[0]
    vlo, vhi = valid[0], valid[1]
    half = rows - EXTRA
    zero = jnp.zeros((PAD, 128), jnp.float32)
    lane = lax.broadcasted_iota(jnp.int32, (8, 128), 1)
    first_lane, last_lane = lane == 0, lane == 127

    def clear(i, carry):
        for ref in (r_v, a_v, b_v):
            for z in range(2):
                ref[i, z, pl.ds(0, PAD), :] = zero
                ref[i, z, pl.ds(PAD + rows, PAD), :] = zero
        return carry

    lax.fori_loop(0, planes + 8, clear, 0)

    def fill(source, first, count):
        def body(p, r):
            for z in range(2):
                r_v[first + p, z, pl.ds(PAD + r, 8), :] = source[p, pl.ds(r, 8), pl.ds(128 * z, 128)]

        sweep_rows(count, tiles, body, UM)

    fill(lo, 0, 4)
    fill(mid, 4, planes)
    fill(hi, planes + 4, 4)

    def smoothed(src, p, row):
        ok = jnp.where(p < 4, vlo, jnp.where(p >= planes + 4, vhi, 1.0))
        c = [src[p, z, pl.ds(row, 8), :] for z in range(2)]
        u0, u1 = pltpu.roll(c[0], 127, 1), pltpu.roll(c[1], 127, 1)
        d0, d1 = pltpu.roll(c[0], 1, 1), pltpu.roll(c[1], 1, 1)
        zs = [
            jnp.where(last_lane, u1, u0) + jnp.where(first_lane, 0.0, d0),
            jnp.where(last_lane, 0.0, u1) + jnp.where(first_lane, d0, d1),
        ]
        new = []
        for z in range(2):
            total = (src[p + 1, z, pl.ds(row, 8), :] + src[p - 1, z, pl.ds(row, 8), :]) + (
                src[p, z, pl.ds(row + 1, 8), :] + src[p, z, pl.ds(row - 1, 8), :]) + zs[z]
            scale = ok * (1.0 / (1.0 + 6.0 * RADIUS_SQ))
            new.append((r_v[p, z, pl.ds(row, 8), :] + RADIUS_SQ * total) * scale)
        return new

    def sweep(src, dst, low, high):
        def body(p, r):
            p, row = low + p, PAD + r
            new = smoothed(src, p, row)
            for z in range(2):
                dst[p, z, pl.ds(row, 8), :] = new[z]

        sweep_rows((high - low), tiles, body, UF)

    sweep(r_v, a_v, 1, planes + 7)
    sweep(a_v, b_v, 2, planes + 6)
    sweep(b_v, a_v, 3, planes + 5)

    skip = h * EXTRA

    def last(p, r):
        new = smoothed(a_v, p + 4, pl.multiple_of(PAD + r + skip, 8))
        for z in range(2):
            out[p, pl.ds(r, 8), pl.ds(128 * z, 128)] = new[z] / dens[p, pl.ds(r, 8), pl.ds(128 * z, 128)]

    sweep_rows(planes, half // 8, last, UF)


def smooth(h, gap, valid, lo, mid, hi, dens):
    planes, rows, cols = mid.shape
    f32 = jnp.float32
    smem = pl.BlockSpec(memory_space=pltpu.SMEM)
    vmem = pl.BlockSpec(memory_space=pltpu.VMEM)

    def kernel(*refs):
        filter_kernel(planes, rows, *refs)

    return pl.pallas_call(
        kernel,
        out_shape=jax.ShapeDtypeStruct(dens.shape, f32),
        in_specs=[smem, smem] + [vmem] * 4,
        out_specs=vmem,
        scratch_shapes=[pltpu.VMEM((planes + 8, 2, rows + 2 * PAD, 128), f32)] * 3,
        compiler_params=pltpu.CompilerParams(vmem_limit_bytes=32 * 1024 * 1024),
        cost_estimate=pl.CostEstimate(flops=5_000_000, bytes_accessed=5_000_000, transcendentals=0),
        name="smooth",
    )(jnp.stack([h, gap]).astype(jnp.int32), valid, lo, mid, hi, dens)


def local(density, support, loads, load_table):
    planes, half, cols = density.shape
    full = loads.shape[2]
    rows = half + EXTRA
    gap = full - rows
    mine = lax.axis_index("case")
    count = lax.axis_size("slab")
    at = lax.axis_index("slab")
    valid = jnp.stack([at > 0, at < count - 1]).astype(jnp.float32)
    rise = [(i, i + 1) for i in range(count - 1)]
    fall = [(i + 1, i) for i in range(count - 1)]
    swap = [(0, 1), (1, 0)]

    partner = lax.ppermute(density, "case", swap)
    lo_c = lax.ppermute(density[planes - 4:], "slab", rise)
    hi_c = lax.ppermute(density[:4], "slab", fall)

    def packed(h):
        own = lax.dynamic_slice_in_dim(loads, h * gap, rows, axis=2)
        sup = lax.dynamic_slice_in_dim(support, h * gap, rows, axis=1)

        def pack(a, b):
            return jnp.concatenate([own[0, a:b], own[1, a:b], sup[a:b]], axis=0)

        return pack(planes - 3, planes), pack(0, 3)

    def exchange(up, down):
        return lax.ppermute(up, "slab", rise), lax.ppermute(down, "slab", fall)

    ints_a = exchange(*packed(1 - mine))
    both = lax.ppermute(jnp.concatenate([lo_c, hi_c]), "case", swap)
    lo_o, hi_o = both[:4], both[4:]
    ints_b = exchange(*packed(mine))
    own = (lo_c, density, hi_c)
    opposite = (lo_o, partner, hi_o)
    u, e_a = step(1 - mine, gap, valid, load_table, loads, support, opposite, own, ints_a, None)
    received = lax.ppermute(e_a, "case", swap)
    u, e_b = step(mine, gap, valid, load_table, loads, support, own, opposite, ints_b, u)
    low = jnp.concatenate([density, partner[:, :EXTRA]], axis=1)
    high = jnp.concatenate([partner[:, half - EXTRA:], density], axis=1)
    mid = jnp.where(mine == 0, low, high)
    right = (-PENALTY * (1.0 - E_MIN)) * (mid * mid * mid) * (e_b + received)
    lo_r, hi_r = exchange(right[planes - 4:], right[:4])
    filtered = smooth(mine, gap, valid, lo_r, right, hi_r, density)
    return u, filtered


def solution(mesh):
    return jax.shard_map(
        local,
        mesh=mesh,
        in_specs=(
            P("slab", "case", None),
            P("slab", None, None),
            P("case", "slab", None, None),
            P(),
        ),
        out_specs=(P("case", None, "slab", None, None), P("slab", "case", None)),
        check_vma=False,
    )
```

```python
import jax
import jax.numpy as jnp
from jax import lax
from jax.experimental import pallas as pl
from jax.experimental.pallas import tpu as pltpu
from jax.sharding import PartitionSpec as P

ITERS = 3
FSWEEPS = 4

E_MIN = 0.001
PENALTY = 3.0
SPRING = 4.0
LOWER = 0.05
UPPER = 2.0
RADIUS_SQ = 2.0

CENTRE = (UPPER + LOWER) / 2.0
HALF = (UPPER - LOWER) / 2.0
SIGMA = CENTRE / HALF
RHO0 = 1.0 / SIGMA
RHO1 = 1.0 / (2.0 * SIGMA - RHO0)
RHO2 = 1.0 / (2.0 * SIGMA - RHO1)
ALPHA1, B1 = RHO1 * RHO0, 2.0 * RHO1 / HALF
ALPHA2, B2 = RHO2 * RHO1, 2.0 * RHO2 / HALF
G0 = ALPHA1 + B1 * (CENTRE - 1.0)
A0 = 1.0 - B2 * ALPHA1 / B1
A1 = 1.0 + ALPHA2 + B2 / B1 - B2
RATIO = B2 / B1

HALO = 4
EXTRA = 8
PAD = 8


def over_rows(tiles, body):
    lax.fori_loop(0, tiles, lambda j, c: body(pl.multiple_of(j * 8, 8)), None, unroll=True)


def step_kernel(planes, rows, info, table, valid, loads, support, lo_d, mid, hi_d, lo_x, mid_x, hi_x, lo_i, hi_i, *rest):
    lo_s, hi_s = rest[:2] if len(rest) > 14 else (None, None)
    (u_out, e_out, d_v, idx_v, sup_v, m_v, k_v, s0_v, s1_v, u_v, in_sem, out_sem) = rest[-12:]
    tiles = rows // 8
    h = info[0]
    vlo, vhi = valid[0], valid[1]
    start = pl.multiple_of(h * info[1], 8)
    wide = planes + 6
    half = rows - EXTRA
    skip = pl.multiple_of(h * EXTRA, 8)

    def density_copies(j):
        own, other, at, count = (
            (lo_d, lo_x, 0, 4), (mid, mid_x, 4, planes), (hi_d, hi_x, planes + 4, 4))[j]
        edge = pl.ds(pl.multiple_of(h * (half - EXTRA), 8), EXTRA)
        beyond = pl.ds(pl.multiple_of((1 - h) * half, 8), EXTRA)
        return [
            pltpu.make_async_copy(own, d_v.at[pl.ds(at, count), pl.ds(skip, half), :], in_sem.at[2 * j]),
            pltpu.make_async_copy(other.at[:, edge, :], d_v.at[pl.ds(at, count), beyond, :], in_sem.at[2 * j + 1]),
        ]

    def halo_copies(j):
        source, shared, at = ((lo_i, lo_s, 0), (hi_i, hi_s, planes + 3))[j]
        made = []
        for part in range(3):
            goal = (idx_v.at[0], idx_v.at[1], sup_v)[part].at[pl.ds(at, 3)]
            group = pl.ds(3 * part, 3)
            sem = 6 + 6 * j + 2 * part
            if lo_s is None:
                made.append(pltpu.make_async_copy(source.at[group], goal, in_sem.at[sem]))
                continue
            fresh, common = rows - 2 * EXTRA, 2 * EXTRA
            made.append(pltpu.make_async_copy(
                source.at[group], goal.at[:, pl.ds(pl.multiple_of(h * common, 8), fresh), :], in_sem.at[sem]))
            made.append(pltpu.make_async_copy(
                shared.at[group, pl.ds(pl.multiple_of(h * fresh, 8), common), :],
                goal.at[:, pl.ds(pl.multiple_of((1 - h) * fresh, 8), common), :], in_sem.at[sem + 1]))
        return made

    def plane_copies(p):
        span = pl.ds(start, rows)
        sem = 18 + 3 * p
        return [
            pltpu.make_async_copy(loads.at[0, p, span, :], idx_v.at[0, p + 3], in_sem.at[sem]),
            pltpu.make_async_copy(loads.at[1, p, span, :], idx_v.at[1, p + 3], in_sem.at[sem + 1]),
            pltpu.make_async_copy(support.at[p, span, :], sup_v.at[p + 3], in_sem.at[sem + 2]),
        ]

    copies = density_copies(0) + density_copies(1) + halo_copies(0)
    for p in range(planes):
        copies += plane_copies(p)
    for copy in copies + density_copies(2) + halo_copies(1):
        copy.start()

    zero = jnp.zeros((PAD, 128), jnp.float32)

    def clear(count, ref):
        def body(i, carry):
            for z in range(2):
                ref[i, z, pl.ds(0, PAD), :] = zero
                ref[i, z, pl.ds(PAD + rows, PAD), :] = zero
            return carry

        lax.fori_loop(0, count, body, 0, unroll=4)

    clear(planes + 8, m_v)
    clear(6 * (planes + 6), s0_v)
    clear(6 * (planes + 4), s1_v)
    clear(6 * (planes + 2), u_v)

    lane = lax.broadcasted_iota(jnp.int32, (8, 128), 1)
    first_lane, last_lane = lane == 0, lane == 127

    def above(a):
        r0, r1 = pltpu.roll(a[0], 127, 1), pltpu.roll(a[1], 127, 1)
        return [jnp.where(last_lane, r1, r0), r1]

    def below(a):
        r0, r1 = pltpu.roll(a[0], 1, 1), pltpu.roll(a[1], 1, 1)
        return [r0, jnp.where(first_lane, r0, r1)]

    def get(ref, i, row):
        return [ref[i, z, pl.ds(row, 8), :] for z in range(2)]

    def modulus(p):
        ok = jnp.where(p < 4, vlo, jnp.where(p >= planes + 4, vhi, 1.0))

        def body(r):
            for z in range(2):
                d = d_v[p, pl.ds(r, 8), pl.ds(128 * z, 128)]
                m_v[p, z, pl.ds(PAD + r, 8), :] = (E_MIN + d * d * d * (1.0 - E_MIN)) * ok

        over_rows(tiles, body)

    def first(p):
        ok = jnp.where(p < 3, vlo, jnp.where(p >= planes + 3, vhi, 1.0))

        def body(r):
            row = PAD + r
            m = get(m_v, p + 1, row)
            zup, zdn = above(m), below(m)
            zup[1] = jnp.where(last_lane, 0.0, zup[1])
            zdn[0] = jnp.where(first_lane, 0.0, zdn[0])
            beside = [get(m_v, p + 2, row), get(m_v, p, row), get(m_v, p + 1, row + 1), get(m_v, p + 1, row - 1), zup, zdn]
            stores = []
            for z in range(2):
                face = [m[z] + b[z] for b in beside]
                double = ((face[0] + face[1]) + (face[2] + face[3])) + (face[4] + face[5])
                diagonal = 0.5 * double + SPRING * sup_v[p, pl.ds(r, 8), pl.ds(128 * z, 128)].astype(jnp.float32)
                w = ok / (diagonal + (1.0 - ok))
                wb = w * (0.5 * B1)
                weight = [f * wb for f in face]
                if z == 1:
                    weight[4] = jnp.where(last_lane, 0.0, weight[4])
                else:
                    weight[5] = jnp.where(first_lane, 0.0, weight[5])
                scale = w * (RATIO / CENTRE)
                for case in range(2):
                    index = idx_v[case, p, pl.ds(r, 8), pl.ds(128 * z, 128)]
                    b0, b1, b2 = (index & 1) != 0, (index & 2) != 0, (index & 4) != 0
                    forces = []
                    for c in range(3):
                        q = [jnp.where(b0, table[2 * j + 1, c], table[2 * j, c]) for j in range(4)]
                        forces.append(jnp.where(b2, jnp.where(b1, q[3], q[2]), jnp.where(b1, q[1], q[0])))
                    for c in range(3):
                        stores.append((s0_v, (p * 6 + case * 3 + c, z, pl.ds(row, 8)), forces[c] * scale))
                for j in range(6):
                    stores.append((k_v, (p, j, z, pl.ds(r, 8)), weight[j]))
            for ref, at, value in stores:
                ref[at] = value

        over_rows(tiles, body)

    def stencil(ref, at, row, k):
        c = get(ref, at, row)
        parts = [get(ref, at + 6, row), get(ref, at - 6, row), get(ref, at, row + 1), get(ref, at, row - 1), above(c), below(c)]
        out = []
        for z in range(2):
            t = [k[j][z] * parts[j][z] for j in range(6)]
            out.append(((t[0] + t[1]) + (t[2] + t[3])) + (t[4] + t[5]))
        return c, out

    def second(p):
        def body(r):
            row = PAD + r
            k = [[k_v[p + 1, j, z, pl.ds(r, 8), :] for z in range(2)] for j in range(6)]
            new = []
            for f in range(6):
                c, t = stencil(s0_v, (p + 1) * 6 + f, row, k)
                new.append([G0 * c[z] + t[z] for z in range(2)])
            for f in range(6):
                for z in range(2):
                    s1_v[p * 6 + f, z, pl.ds(row, 8), :] = new[f][z]

        over_rows(tiles, body)

    def third(p):
        def body(r):
            row = PAD + r
            k = [[k_v[p + 2, j, z, pl.ds(r, 8), :] for z in range(2)] for j in range(6)]
            new = []
            for f in range(6):
                c, t = stencil(s1_v, (p + 1) * 6 + f, row, k)
                base = get(s0_v, (p + 2) * 6 + f, row)
                new.append([(A0 / RATIO) * base[z] + (A1 / RATIO) * c[z] + t[z] for z in range(2)])
            for f in range(6):
                for z in range(2):
                    u_v[p * 6 + f, z, pl.ds(row, 8), :] = new[f][z]

        over_rows(tiles, body)

    def out_copies(p):
        return [
            pltpu.make_async_copy(
                u_v.at[(p + 1) * 6 + f, z, pl.ds(PAD + skip, half), :],
                u_out.at[f // 3, f % 3, p, pl.ds(pl.multiple_of(h * half, 8), half), pl.ds(128 * z, 128)],
                out_sem.at[p * 12 + f * 2 + z])
            for f in range(6) for z in range(2)
        ]

    def energy(p):
        def body(r):
            row = PAD + r
            acc = [[], []]
            for f in range(6):
                at = (p + 1) * 6 + f
                c = get(u_v, at, row)
                zup, zdn = above(c), below(c)
                zup[1] = jnp.where(last_lane, 0.0, zup[1])
                zdn[0] = jnp.where(first_lane, 0.0, zdn[0])
                for b in (get(u_v, at + 6, row), get(u_v, at - 6, row), get(u_v, at, row + 1), get(u_v, at, row - 1), zup, zdn):
                    for z in range(2):
                        d = c[z] - b[z]
                        if len(acc[z]) < 3:
                            acc[z].append(d * d)
                        else:
                            acc[z] = acc[z][1:] + [acc[z][0] + d * d]
            for z in range(2):
                e_out[p, pl.ds(r, 8), pl.ds(128 * z, 128)] = 0.5 * (acc[z][0] + acc[z][1] + acc[z][2])

        over_rows(tiles, body)

    for copy in density_copies(0) + density_copies(1):
        copy.wait()
    modulus(0)
    modulus(1)

    def each(count, body):
        def go(p, carry):
            body(p)
            return carry

        lax.fori_loop(0, count, go, 0)

    for copy in density_copies(2):
        copy.wait()
    each(planes + 6, lambda p: modulus(p + 2))
    for copy in halo_copies(0) + halo_copies(1):
        copy.wait()
    for p in range(planes):
        for copy in plane_copies(p):
            copy.wait()
    each(planes + 6, first)
    each(planes + 4, second)
    each(planes + 2, third)
    for p in range(planes):
        for copy in out_copies(p):
            copy.start()
    each(planes, energy)
    for p in range(planes):
        for copy in out_copies(p):
            copy.wait()


def step(h, gap, valid, table, loads, support, main, other, ints, u):
    planes, half, cols = main[1].shape
    rows = half + EXTRA
    tiles_rows = rows + 2 * PAD
    f32 = jnp.float32
    any_spec = pl.BlockSpec(memory_space=pl.ANY)
    smem = pl.BlockSpec(memory_space=pltpu.SMEM)
    vmem = pl.BlockSpec(memory_space=pltpu.VMEM)
    full = loads.shape[2]
    args = [jnp.stack([h, gap]).astype(jnp.int32), table, valid, loads, support, *main, *other, *ints]
    specs = [smem, smem, smem] + [any_spec] * (len(args) - 3)
    aliases = {}
    if u is not None:
        args.append(u)
        specs.append(any_spec)
        aliases = {len(args) - 1: 0}

    def kernel(*refs):
        step_kernel(planes, rows, *refs)

    return pl.pallas_call(
        kernel,
        out_shape=(jax.ShapeDtypeStruct((2, 3, planes, full, cols), f32), jax.ShapeDtypeStruct((planes, rows, cols), f32)),
        in_specs=specs,
        out_specs=(any_spec, vmem),
        input_output_aliases=aliases,
        scratch_shapes=[
            pltpu.VMEM((planes + 8, rows, cols), f32),
            pltpu.VMEM((2, planes + 6, rows, cols), jnp.int32),
            pltpu.VMEM((planes + 6, rows, cols), jnp.int32),
            pltpu.VMEM((planes + 8, 2, tiles_rows, 128), f32),
            pltpu.VMEM((planes + 6, 6, 2, rows, 128), f32),
            pltpu.VMEM((6 * (planes + 6), 2, tiles_rows, 128), f32),
            pltpu.VMEM((6 * (planes + 4), 2, tiles_rows, 128), f32),
            pltpu.VMEM((6 * (planes + 2), 2, tiles_rows, 128), f32),
            pltpu.SemaphoreType.DMA((18 + 3 * planes,)),
            pltpu.SemaphoreType.DMA((12 * planes,)),
        ],
        compiler_params=pltpu.CompilerParams(vmem_limit_bytes=56 * 1024 * 1024),
        cost_estimate=pl.CostEstimate(flops=40_000_000, bytes_accessed=40_000_000, transcendentals=0),
        name="relax",
    )(*args)


def filter_kernel(planes, rows, info, valid, lo, mid, hi, dens, out, r_v, a_v, b_v):
    tiles = rows // 8
    h = info[0]
    vlo, vhi = valid[0], valid[1]
    half = rows - EXTRA
    zero = jnp.zeros((PAD, 128), jnp.float32)
    lane = lax.broadcasted_iota(jnp.int32, (8, 128), 1)
    first_lane, last_lane = lane == 0, lane == 127

    def clear(i, carry):
        for ref in (r_v, a_v, b_v):
            for z in range(2):
                ref[i, z, pl.ds(0, PAD), :] = zero
                ref[i, z, pl.ds(PAD + rows, PAD), :] = zero
        return carry

    lax.fori_loop(0, planes + 8, clear, 0, unroll=4)

    def batches(total, body):
        for at in range(0, total, 5):
            body([8 * j for j in range(at, min(at + 5, total))])

    def fill(source, at, count):
        def plane(p, carry):
            def body(offsets):
                new = [[source[p, pl.ds(r, 8), pl.ds(128 * z, 128)] for z in range(2)] for r in offsets]
                for r, v in zip(offsets, new):
                    for z in range(2):
                        r_v[at + p, z, pl.ds(PAD + r, 8), :] = v[z]

            batches(tiles, body)
            return carry

        lax.fori_loop(0, count, plane, 0)

    fill(lo, 0, 4)
    fill(mid, 4, planes)
    fill(hi, planes + 4, 4)

    def smoothed(src, p, row, scale):
        c = [src[p, z, pl.ds(row, 8), :] for z in range(2)]
        u0, u1 = pltpu.roll(c[0], 127, 1), pltpu.roll(c[1], 127, 1)
        d0, d1 = pltpu.roll(c[0], 1, 1), pltpu.roll(c[1], 1, 1)
        zs = [
            jnp.where(last_lane, u1, u0) + jnp.where(first_lane, 0.0, d0),
            jnp.where(last_lane, 0.0, u1) + jnp.where(first_lane, d0, d1),
        ]
        new = []
        for z in range(2):
            total = (src[p + 1, z, pl.ds(row, 8), :] + src[p - 1, z, pl.ds(row, 8), :]) + (
                src[p, z, pl.ds(row + 1, 8), :] + src[p, z, pl.ds(row - 1, 8), :]) + zs[z]
            new.append((r_v[p, z, pl.ds(row, 8), :] + RADIUS_SQ * total) * scale)
        return new

    def sweep(src, dst, low, high):
        def plane(i, carry):
            p = low + i
            ok = jnp.where(p < 4, vlo, jnp.where(p >= planes + 4, vhi, 1.0))
            scale = ok * (1.0 / (1.0 + 6.0 * RADIUS_SQ))

            def body(offsets):
                new = [smoothed(src, p, pl.multiple_of(PAD + r, 8) if not isinstance(r, int) else PAD + r, scale) for r in offsets]
                for r, v in zip(offsets, new):
                    for z in range(2):
                        dst[p, z, pl.ds(PAD + r, 8), :] = v[z]

            batches(tiles, body)
            return carry

        lax.fori_loop(0, high - low, plane, 0)

    sweep(r_v, a_v, 1, planes + 7)
    sweep(a_v, b_v, 2, planes + 6)
    sweep(b_v, a_v, 3, planes + 5)

    skip = pl.multiple_of(h * EXTRA, 8)

    def last(p, carry):
        def body(offsets):
            new = [smoothed(a_v, p + 4, pl.multiple_of(PAD + r + skip, 8), 1.0 / (1.0 + 6.0 * RADIUS_SQ)) for r in offsets]
            for r, v in zip(offsets, new):
                for z in range(2):
                    out[p, pl.ds(r, 8), pl.ds(128 * z, 128)] = v[z] / dens[p, pl.ds(r, 8), pl.ds(128 * z, 128)]

        batches(half // 8, body)
        return carry

    lax.fori_loop(0, planes, last, 0)


def smooth(h, gap, valid, lo, mid, hi, dens):
    planes, rows, cols = mid.shape
    f32 = jnp.float32
    smem = pl.BlockSpec(memory_space=pltpu.SMEM)
    vmem = pl.BlockSpec(memory_space=pltpu.VMEM)

    def kernel(*refs):
        filter_kernel(planes, rows, *refs)

    return pl.pallas_call(
        kernel,
        out_shape=jax.ShapeDtypeStruct(dens.shape, f32),
        in_specs=[smem, smem] + [vmem] * 4,
        out_specs=vmem,
        scratch_shapes=[pltpu.VMEM((planes + 8, 2, rows + 2 * PAD, 128), f32)] * 3,
        compiler_params=pltpu.CompilerParams(vmem_limit_bytes=32 * 1024 * 1024),
        cost_estimate=pl.CostEstimate(flops=5_000_000, bytes_accessed=5_000_000, transcendentals=0),
        name="smooth",
    )(jnp.stack([h, gap]).astype(jnp.int32), valid, lo, mid, hi, dens)


def local(density, support, loads, load_table):
    planes, half, cols = density.shape
    full = loads.shape[2]
    rows = half + EXTRA
    gap = full - rows
    mine = lax.axis_index("case")
    count = lax.axis_size("slab")
    at = lax.axis_index("slab")
    valid = jnp.stack([at > 0, at < count - 1]).astype(jnp.float32)
    rise = [(i, i + 1) for i in range(count - 1)]
    fall = [(i + 1, i) for i in range(count - 1)]
    swap = [(0, 1), (1, 0)]

    partner = lax.ppermute(density, "case", swap)
    lo_c = lax.ppermute(density[planes - 4:], "slab", rise)
    hi_c = lax.ppermute(density[:4], "slab", fall)

    def packed(start, length):
        own = lax.dynamic_slice_in_dim(loads, start, length, axis=2)
        sup = lax.dynamic_slice_in_dim(support, start, length, axis=1)

        def pack(a, b):
            return jnp.concatenate([own[0, a:b], own[1, a:b], sup[a:b]], axis=0)

        return pack(planes - 3, planes), pack(0, 3)

    def exchange(up, down):
        return lax.ppermute(up, "slab", rise), lax.ppermute(down, "slab", fall)

    payload_a = packed((1 - mine) * gap, rows)
    payload_b = packed(mine * rows, rows - 2 * EXTRA)
    ints_a = exchange(*payload_a)
    lo_c, hi_c, partner, _ = lax.optimization_barrier((lo_c, hi_c, partner, payload_a))
    both = lax.ppermute(jnp.concatenate([lo_c, hi_c]), "case", swap)
    both, payload_b = lax.optimization_barrier((both, payload_b))
    lo_o, hi_o = both[:4], both[4:]
    ints_b = exchange(*payload_b) + ints_a
    own = (lo_c, density, hi_c)
    opposite = (lo_o, partner, hi_o)
    u, e_a = step(1 - mine, gap, valid, load_table, loads, support, opposite, own, ints_a, None)
    received = lax.ppermute(e_a, "case", swap)
    u, e_b = step(mine, gap, valid, load_table, loads, support, own, opposite, ints_b, u)
    low = jnp.concatenate([density, partner[:, :EXTRA]], axis=1)
    high = jnp.concatenate([partner[:, half - EXTRA:], density], axis=1)
    mid = jnp.where(mine == 0, low, high)
    right = (-PENALTY * (1.0 - E_MIN)) * (mid * mid * mid) * (e_b + received)
    lo_r, hi_r = exchange(right[planes - 4:], right[:4])
    filtered = smooth(mine, gap, valid, lo_r, right, hi_r, density)
    return u, filtered


def solution(mesh):
    return jax.shard_map(
        local,
        mesh=mesh,
        in_specs=(
            P("slab", "case", None),
            P("slab", None, None),
            P("case", "slab", None, None),
            P(),
        ),
        out_specs=(P("case", None, "slab", None, None), P("slab", "case", None)),
        check_vma=False,
    )
```

```python
import jax
import jax.numpy as jnp
from jax import lax
from jax.experimental import pallas as pl
from jax.experimental.pallas import tpu as pltpu
from jax.sharding import PartitionSpec as P

ITERS = 3
FSWEEPS = 4

E_MIN = 0.001
PENALTY = 3.0
SPRING = 4.0
LOWER = 0.05
UPPER = 2.0
RADIUS_SQ = 2.0

CENTRE = (UPPER + LOWER) / 2.0
HALF = (UPPER - LOWER) / 2.0
SIGMA = CENTRE / HALF
RHO0 = 1.0 / SIGMA
RHO1 = 1.0 / (2.0 * SIGMA - RHO0)
RHO2 = 1.0 / (2.0 * SIGMA - RHO1)
ALPHA1, B1 = RHO1 * RHO0, 2.0 * RHO1 / HALF
ALPHA2, B2 = RHO2 * RHO1, 2.0 * RHO2 / HALF
G0 = ALPHA1 + B1 * (CENTRE - 1.0)
A0 = 1.0 - B2 * ALPHA1 / B1
A1 = 1.0 + ALPHA2 + B2 / B1 - B2
RATIO = B2 / B1

HALO = 4
EXTRA = 8
PAD = 8


def over_rows(tiles, body):
    lax.fori_loop(0, tiles, lambda j, c: body(pl.multiple_of(j * 8, 8)), None, unroll=True)


def over_planes(count, body):
    def go(p, carry):
        body(p)
        return carry

    lax.fori_loop(0, count, go, 0)


def step_kernel(planes, rows, info, table, valid, loads, support, lo_d, mid, hi_d, edge_v, lo_i, hi_i, *rest):
    lo_s, hi_s = rest[:2] if len(rest) > 12 else (None, None)
    (u_out, e_out, idx_v, sup_v, m_v, k_v, s0_v, s1_v, u_v, in_sem, out_sem) = rest[-11:]
    tiles = rows // 8
    h = info[0]
    vlo, vhi = valid[0], valid[1]
    start = pl.multiple_of(h * info[1], 8)
    half = rows - EXTRA
    skip = pl.multiple_of(h * EXTRA, 8)
    fresh, common = rows - 2 * EXTRA, 2 * EXTRA

    span = pl.ds(start, rows)
    owned = [
        pltpu.make_async_copy(loads.at[0, :, span, :], idx_v.at[0], in_sem.at[0]),
        pltpu.make_async_copy(loads.at[1, :, span, :], idx_v.at[1], in_sem.at[1]),
        pltpu.make_async_copy(support.at[:, span, :], sup_v, in_sem.at[2]),
    ]
    for copy in owned:
        copy.start()

    zero = jnp.zeros((PAD, 128), jnp.float32)

    def clear(count, ref):
        def body(i, carry):
            for z in range(2):
                ref[i, z, pl.ds(0, PAD), :] = zero
                ref[i, z, pl.ds(PAD + rows, PAD), :] = zero
            return carry

        lax.fori_loop(0, count, body, 0, unroll=4)

    clear(planes + 8, m_v)
    clear(6 * (planes + 6), s0_v)
    clear(6 * (planes + 4), s1_v)
    clear(6 * (planes + 2), u_v)

    lane = lax.broadcasted_iota(jnp.int32, (8, 128), 1)
    first_lane, last_lane = lane == 0, lane == 127

    def above(a):
        r0, r1 = pltpu.roll(a[0], 127, 1), pltpu.roll(a[1], 127, 1)
        return [jnp.where(last_lane, r1, r0), r1]

    def below(a):
        r0, r1 = pltpu.roll(a[0], 1, 1), pltpu.roll(a[1], 1, 1)
        return [r0, jnp.where(first_lane, r0, r1)]

    def get(ref, i, row):
        return [ref[i, z, pl.ds(row, 8), :] for z in range(2)]

    def moduli(own, at, count, ok):
        def plane(p):
            def put(source, r, row):
                for z in range(2):
                    d = source[p, pl.ds(r, 8), pl.ds(128 * z, 128)]
                    m_v[at + p, z, pl.ds(pl.multiple_of(PAD + row, 8), 8), :] = (E_MIN + d * d * d * (1.0 - E_MIN)) * ok

            def put_edge(p):
                for z in range(2):
                    d = edge_v[at + p, :, pl.ds(128 * z, 128)]
                    m_v[at + p, z, pl.ds(pl.multiple_of(PAD + (1 - h) * half, 8), 8), :] = (E_MIN + d * d * d * (1.0 - E_MIN)) * ok

            over_rows(half // 8, lambda r: put(own, r, skip + r))
            put_edge(p)

        over_planes(count, plane)

    def first(p, r, ok, index_at, support_at):
        r = pl.multiple_of(r, 8)
        row = pl.multiple_of(PAD + r, 8)
        m = get(m_v, p + 1, row)
        zup, zdn = above(m), below(m)
        zup[1] = jnp.where(last_lane, 0.0, zup[1])
        zdn[0] = jnp.where(first_lane, 0.0, zdn[0])
        beside = [get(m_v, p + 2, row), get(m_v, p, row), get(m_v, p + 1, row + 1), get(m_v, p + 1, row - 1), zup, zdn]
        stores = []
        for z in range(2):
            face = [m[z] + b[z] for b in beside]
            double = ((face[0] + face[1]) + (face[2] + face[3])) + (face[4] + face[5])
            diagonal = 0.5 * double + SPRING * support_at(z).astype(jnp.float32)
            w = ok / (diagonal + (1.0 - ok))
            wb = w * (0.5 * B1)
            weight = [f * wb for f in face]
            if z == 1:
                weight[4] = jnp.where(last_lane, 0.0, weight[4])
            else:
                weight[5] = jnp.where(first_lane, 0.0, weight[5])
            scale = w * (RATIO / CENTRE)
            for case in range(2):
                index = index_at(case, z)
                b0, b1, b2 = (index & 1) != 0, (index & 2) != 0, (index & 4) != 0
                forces = []
                for c in range(3):
                    q = [jnp.where(b0, table[2 * j + 1, c], table[2 * j, c]) for j in range(4)]
                    forces.append(jnp.where(b2, jnp.where(b1, q[3], q[2]), jnp.where(b1, q[1], q[0])))
                for c in range(3):
                    stores.append((s0_v, (p * 6 + case * 3 + c, z, pl.ds(row, 8)), forces[c] * scale))
            for j in range(6):
                stores.append((k_v, (p, j, z, pl.ds(r, 8)), weight[j]))
        for ref, at, value in stores:
            ref[at] = value

    def first_halo(source, side, at, ok):
        def from_source(p, ref, r, row):
            def cut(i, z):
                return ref[i, pl.ds(pl.multiple_of(r, 8), 8), pl.ds(128 * z, 128)]

            first(at + p, row, ok, lambda case, z: cut(3 * case + p, z), lambda z: cut(6 + p, z))

        def plane(p):
            if lo_s is None:
                over_rows(tiles, lambda r: from_source(p, source, r, r))
            else:
                over_rows(fresh // 8, lambda r: from_source(p, source, r, h * common + r))
                over_rows(common // 8, lambda r: from_source(p, (lo_s, hi_s)[side], r, (1 - h) * fresh + r))

        over_planes(3, plane)

    def first_own(p):
        def body(r):
            first(
                p + 3, r, 1.0,
                lambda case, z: idx_v[case, p, pl.ds(r, 8), pl.ds(128 * z, 128)],
                lambda z: sup_v[p, pl.ds(r, 8), pl.ds(128 * z, 128)])

        over_rows(tiles, body)

    def stencil(ref, at, row, k):
        c = get(ref, at, row)
        parts = [get(ref, at + 6, row), get(ref, at - 6, row), get(ref, at, row + 1), get(ref, at, row - 1), above(c), below(c)]
        out = []
        for z in range(2):
            t = [k[j][z] * parts[j][z] for j in range(6)]
            out.append(((t[0] + t[1]) + (t[2] + t[3])) + (t[4] + t[5]))
        return c, out

    def second(p):
        def body(r):
            row = PAD + r
            k = [[k_v[p + 1, j, z, pl.ds(r, 8), :] for z in range(2)] for j in range(6)]
            new = []
            for f in range(6):
                c, t = stencil(s0_v, (p + 1) * 6 + f, row, k)
                new.append([G0 * c[z] + t[z] for z in range(2)])
            for f in range(6):
                for z in range(2):
                    s1_v[p * 6 + f, z, pl.ds(row, 8), :] = new[f][z]

        over_rows(tiles, body)

    def third(p):
        def body(r):
            row = PAD + r
            k = [[k_v[p + 2, j, z, pl.ds(r, 8), :] for z in range(2)] for j in range(6)]
            new = []
            for f in range(6):
                c, t = stencil(s1_v, (p + 1) * 6 + f, row, k)
                base = get(s0_v, (p + 2) * 6 + f, row)
                new.append([(A0 / RATIO) * base[z] + (A1 / RATIO) * c[z] + t[z] for z in range(2)])
            for f in range(6):
                for z in range(2):
                    u_v[p * 6 + f, z, pl.ds(row, 8), :] = new[f][z]

        over_rows(tiles, body)

    def out_copies(p):
        return [
            pltpu.make_async_copy(
                u_v.at[(p + 1) * 6 + f, z, pl.ds(PAD + skip, half), :],
                u_out.at[f // 3, f % 3, p, pl.ds(pl.multiple_of(h * half, 8), half), pl.ds(128 * z, 128)],
                out_sem.at[p * 12 + f * 2 + z])
            for f in range(6) for z in range(2)
        ]

    def energy(p):
        def body(r):
            row = PAD + r
            acc = [[], []]
            for f in range(6):
                at = (p + 1) * 6 + f
                c = get(u_v, at, row)
                zup, zdn = above(c), below(c)
                zup[1] = jnp.where(last_lane, 0.0, zup[1])
                zdn[0] = jnp.where(first_lane, 0.0, zdn[0])
                for b in (get(u_v, at + 6, row), get(u_v, at - 6, row), get(u_v, at, row + 1), get(u_v, at, row - 1), zup, zdn):
                    for z in range(2):
                        d = c[z] - b[z]
                        if len(acc[z]) < 3:
                            acc[z].append(d * d)
                        else:
                            acc[z] = acc[z][1:] + [acc[z][0] + d * d]
            for z in range(2):
                e_out[p, pl.ds(r, 8), pl.ds(128 * z, 128)] = 0.5 * (acc[z][0] + acc[z][1] + acc[z][2])

        over_rows(tiles, body)

    moduli(lo_d, 0, 4, vlo)
    moduli(mid, 4, planes, 1.0)
    moduli(hi_d, planes + 4, 4, vhi)
    first_halo(lo_i, 0, 0, vlo)
    first_halo(hi_i, 1, planes + 3, vhi)
    for copy in owned:
        copy.wait()
    over_planes(planes, first_own)
    over_planes(planes + 4, second)
    over_planes(planes + 2, third)
    for p in range(planes):
        for copy in out_copies(p):
            copy.start()
    over_planes(planes, energy)
    for p in range(planes):
        for copy in out_copies(p):
            copy.wait()


def step(h, gap, valid, table, loads, support, main, edge, ints, u):
    planes, half, cols = main[1].shape
    rows = half + EXTRA
    tiles_rows = rows + 2 * PAD
    f32 = jnp.float32
    any_spec = pl.BlockSpec(memory_space=pl.ANY)
    smem = pl.BlockSpec(memory_space=pltpu.SMEM)
    vmem = pl.BlockSpec(memory_space=pltpu.VMEM)
    full = loads.shape[2]
    args = [jnp.stack([h, gap]).astype(jnp.int32), table, valid, loads, support, *main, edge, *ints]
    specs = [smem] * 3 + [pl.BlockSpec(memory_space=pltpu.HBM)] * 2 + [vmem] * (len(args) - 5)
    aliases = {}
    if u is not None:
        args.append(u)
        specs.append(any_spec)
        aliases = {len(args) - 1: 0}

    def kernel(*refs):
        step_kernel(planes, rows, *refs)

    return pl.pallas_call(
        kernel,
        out_shape=(jax.ShapeDtypeStruct((2, 3, planes, full, cols), f32), jax.ShapeDtypeStruct((planes, rows, cols), f32)),
        in_specs=specs,
        out_specs=(any_spec, vmem),
        input_output_aliases=aliases,
        scratch_shapes=[
            pltpu.VMEM((2, planes, rows, cols), jnp.int32),
            pltpu.VMEM((planes, rows, cols), jnp.int32),
            pltpu.VMEM((planes + 8, 2, tiles_rows, 128), f32),
            pltpu.VMEM((planes + 6, 6, 2, rows, 128), f32),
            pltpu.VMEM((6 * (planes + 6), 2, tiles_rows, 128), f32),
            pltpu.VMEM((6 * (planes + 4), 2, tiles_rows, 128), f32),
            pltpu.VMEM((6 * (planes + 2), 2, tiles_rows, 128), f32),
            pltpu.SemaphoreType.DMA((3,)),
            pltpu.SemaphoreType.DMA((12 * planes,)),
        ],
        compiler_params=pltpu.CompilerParams(vmem_limit_bytes=42 * 1024 * 1024),
        cost_estimate=pl.CostEstimate(flops=40_000_000, bytes_accessed=40_000_000, transcendentals=0),
        name="relax",
    )(*args)


def filter_kernel(planes, rows, info, valid, lo, mid, hi, dens, out, r_v, a_v, b_v):
    tiles = rows // 8
    h = info[0]
    vlo, vhi = valid[0], valid[1]
    half = rows - EXTRA
    zero = jnp.zeros((PAD, 128), jnp.float32)
    lane = lax.broadcasted_iota(jnp.int32, (8, 128), 1)
    first_lane, last_lane = lane == 0, lane == 127

    def clear(i, carry):
        for ref in (r_v, a_v, b_v):
            for z in range(2):
                ref[i, z, pl.ds(0, PAD), :] = zero
                ref[i, z, pl.ds(PAD + rows, PAD), :] = zero
        return carry

    lax.fori_loop(0, planes + 8, clear, 0, unroll=4)

    def batches(total, body):
        for at in range(0, total, 5):
            body([8 * j for j in range(at, min(at + 5, total))])

    def fill(source, at, count):
        def plane(p, carry):
            def body(offsets):
                new = [[source[p, pl.ds(r, 8), pl.ds(128 * z, 128)] for z in range(2)] for r in offsets]
                for r, v in zip(offsets, new):
                    for z in range(2):
                        r_v[at + p, z, pl.ds(PAD + r, 8), :] = v[z]

            batches(tiles, body)
            return carry

        lax.fori_loop(0, count, plane, 0)

    fill(lo, 0, 4)
    fill(mid, 4, planes)
    fill(hi, planes + 4, 4)

    def smoothed(src, p, row, scale):
        c = [src[p, z, pl.ds(row, 8), :] for z in range(2)]
        u0, u1 = pltpu.roll(c[0], 127, 1), pltpu.roll(c[1], 127, 1)
        d0, d1 = pltpu.roll(c[0], 1, 1), pltpu.roll(c[1], 1, 1)
        zs = [
            jnp.where(last_lane, u1, u0) + jnp.where(first_lane, 0.0, d0),
            jnp.where(last_lane, 0.0, u1) + jnp.where(first_lane, d0, d1),
        ]
        new = []
        for z in range(2):
            total = (src[p + 1, z, pl.ds(row, 8), :] + src[p - 1, z, pl.ds(row, 8), :]) + (
                src[p, z, pl.ds(row + 1, 8), :] + src[p, z, pl.ds(row - 1, 8), :]) + zs[z]
            new.append((r_v[p, z, pl.ds(row, 8), :] + RADIUS_SQ * total) * scale)
        return new

    def sweep(src, dst, low, high):
        def plane(i, carry):
            p = low + i
            ok = jnp.where(p < 4, vlo, jnp.where(p >= planes + 4, vhi, 1.0))
            scale = ok * (1.0 / (1.0 + 6.0 * RADIUS_SQ))

            def body(offsets):
                new = [smoothed(src, p, pl.multiple_of(PAD + r, 8) if not isinstance(r, int) else PAD + r, scale) for r in offsets]
                for r, v in zip(offsets, new):
                    for z in range(2):
                        dst[p, z, pl.ds(PAD + r, 8), :] = v[z]

            batches(tiles, body)
            return carry

        lax.fori_loop(0, high - low, plane, 0)

    sweep(r_v, a_v, 1, planes + 7)
    sweep(a_v, b_v, 2, planes + 6)
    sweep(b_v, a_v, 3, planes + 5)

    skip = pl.multiple_of(h * EXTRA, 8)

    def last(p, carry):
        def body(offsets):
            new = [smoothed(a_v, p + 4, pl.multiple_of(PAD + r + skip, 8), 1.0 / (1.0 + 6.0 * RADIUS_SQ)) for r in offsets]
            for r, v in zip(offsets, new):
                for z in range(2):
                    out[p, pl.ds(r, 8), pl.ds(128 * z, 128)] = v[z] / dens[p, pl.ds(r, 8), pl.ds(128 * z, 128)]

        batches(half // 8, body)
        return carry

    lax.fori_loop(0, planes, last, 0)


def smooth(h, gap, valid, lo, mid, hi, dens):
    planes, rows, cols = mid.shape
    f32 = jnp.float32
    smem = pl.BlockSpec(memory_space=pltpu.SMEM)
    vmem = pl.BlockSpec(memory_space=pltpu.VMEM)

    def kernel(*refs):
        filter_kernel(planes, rows, *refs)

    return pl.pallas_call(
        kernel,
        out_shape=jax.ShapeDtypeStruct(dens.shape, f32),
        in_specs=[smem, smem] + [vmem] * 4,
        out_specs=vmem,
        scratch_shapes=[pltpu.VMEM((planes + 8, 2, rows + 2 * PAD, 128), f32)] * 3,
        compiler_params=pltpu.CompilerParams(vmem_limit_bytes=32 * 1024 * 1024),
        cost_estimate=pl.CostEstimate(flops=5_000_000, bytes_accessed=5_000_000, transcendentals=0),
        name="smooth",
    )(jnp.stack([h, gap]).astype(jnp.int32), valid, lo, mid, hi, dens)


def local(density, support, loads, load_table):
    planes, half, cols = density.shape
    full = loads.shape[2]
    rows = half + EXTRA
    gap = full - rows
    mine = lax.axis_index("case")
    count = lax.axis_size("slab")
    at = lax.axis_index("slab")
    valid = jnp.stack([at > 0, at < count - 1]).astype(jnp.float32)
    rise = [(i, i + 1) for i in range(count - 1)]
    fall = [(i + 1, i) for i in range(count - 1)]
    swap = [(0, 1), (1, 0)]

    partner = lax.ppermute(density, "case", swap)
    lo_c = lax.ppermute(density[planes - 4:], "slab", rise)
    hi_c = lax.ppermute(density[:4], "slab", fall)

    def packed(start, length):
        own = lax.dynamic_slice_in_dim(loads, start, length, axis=2)
        sup = lax.dynamic_slice_in_dim(support, start, length, axis=1)

        def pack(a, b):
            return jnp.concatenate([own[0, a:b], own[1, a:b], sup[a:b]], axis=0)

        return pack(planes - 3, planes), pack(0, 3)

    def exchange(up, down):
        return lax.ppermute(up, "slab", rise), lax.ppermute(down, "slab", fall)

    payload_a = packed((1 - mine) * gap, rows)
    payload_b = packed(mine * rows, rows - 2 * EXTRA)
    ints_a = exchange(*payload_a)
    lo_c, hi_c, partner, _ = lax.optimization_barrier((lo_c, hi_c, partner, payload_a))
    both = lax.ppermute(jnp.concatenate([lo_c, hi_c]), "case", swap)
    both, payload_b = lax.optimization_barrier((both, payload_b))
    lo_o, hi_o = both[:4], both[4:]
    common = [lax.dynamic_slice_in_dim(v, mine * (rows - 2 * EXTRA), 2 * EXTRA, axis=1) for v in ints_a]
    ints_b = (*exchange(*payload_b), *common)
    own = (lo_c, density, hi_c)
    opposite = (lo_o, partner, hi_o)

    def edge(h, parts):
        return jnp.concatenate([lax.dynamic_slice_in_dim(v, h * (half - EXTRA), EXTRA, axis=1) for v in parts])

    u, e_a = step(1 - mine, gap, valid, load_table, loads, support, opposite, edge(1 - mine, own), ints_a, None)
    received = lax.ppermute(e_a, "case", swap)
    u, e_b = step(mine, gap, valid, load_table, loads, support, own, edge(mine, opposite), ints_b, u)
    low = jnp.concatenate([density, partner[:, :EXTRA]], axis=1)
    high = jnp.concatenate([partner[:, half - EXTRA:], density], axis=1)
    mid = jnp.where(mine == 0, low, high)
    right = (-PENALTY * (1.0 - E_MIN)) * (mid * mid * mid) * (e_b + received)
    lo_r, hi_r = exchange(right[planes - 4:], right[:4])
    filtered = smooth(mine, gap, valid, lo_r, right, hi_r, density)
    return u, filtered


def solution(mesh):
    return jax.shard_map(
        local,
        mesh=mesh,
        in_specs=(
            P("slab", "case", None),
            P("slab", None, None),
            P("case", "slab", None, None),
            P(),
        ),
        out_specs=(P("case", None, "slab", None, None), P("slab", "case", None)),
        check_vma=False,
    )
```

```python
import jax
import jax.numpy as jnp
from jax import lax
from jax.experimental import pallas as pl
from jax.experimental.pallas import tpu as pltpu
from jax.sharding import PartitionSpec as P

ITERS = 3
FSWEEPS = 4

E_MIN = 0.001
PENALTY = 3.0
SPRING = 4.0
LOWER = 0.05
UPPER = 2.0
RADIUS_SQ = 2.0

CENTRE = (UPPER + LOWER) / 2.0
HALF = (UPPER - LOWER) / 2.0
SIGMA = CENTRE / HALF
RHO0 = 1.0 / SIGMA
RHO1 = 1.0 / (2.0 * SIGMA - RHO0)
RHO2 = 1.0 / (2.0 * SIGMA - RHO1)
ALPHA1, B1 = RHO1 * RHO0, 2.0 * RHO1 / HALF
ALPHA2, B2 = RHO2 * RHO1, 2.0 * RHO2 / HALF
G0 = ALPHA1 + B1 * (CENTRE - 1.0)
A0 = 1.0 - B2 * ALPHA1 / B1
A1 = 1.0 + ALPHA2 + B2 / B1 - B2
RATIO = B2 / B1

HALO = 4
EXTRA = 8
PAD = 8


def over_rows(tiles, body):
    lax.fori_loop(0, tiles, lambda j, c: body(pl.multiple_of(j * 8, 8)), None, unroll=True)


def over_planes(count, body):
    def go(p, carry):
        body(p)
        return carry

    lax.fori_loop(0, count, go, 0)


def step_kernel(planes, rows, info, table, valid, loads, support, lo_d, mid, hi_d, edge_v, lo_i, hi_i, *rest):
    lo_s, hi_s, lo_l, hi_l = rest[:4] if len(rest) > 12 else (None,) * 4
    (u_out, e_out, idx_v, sup_v, m_v, k_v, s0_v, s1_v, u_v, in_sem, out_sem) = rest[-11:]
    tiles = rows // 8
    h = info[0]
    vlo, vhi = valid[0], valid[1]
    start = pl.multiple_of(h * info[1], 8)
    half = rows - EXTRA
    skip = pl.multiple_of(h * EXTRA, 8)
    fresh, common = rows - 2 * EXTRA, 2 * EXTRA

    span = pl.ds(start, rows)
    owned = [
        pltpu.make_async_copy(loads.at[0, :, span, :], idx_v.at[0], in_sem.at[0]),
        pltpu.make_async_copy(loads.at[1, :, span, :], idx_v.at[1], in_sem.at[1]),
        pltpu.make_async_copy(support.at[:, span, :], sup_v, in_sem.at[2]),
    ]
    for copy in owned:
        copy.start()

    zero = jnp.zeros((PAD, 128), jnp.float32)

    def clear(count, ref):
        def body(i, carry):
            for z in range(2):
                ref[i, z, pl.ds(0, PAD), :] = zero
                ref[i, z, pl.ds(PAD + rows, PAD), :] = zero
            return carry

        lax.fori_loop(0, count, body, 0, unroll=4)

    clear(planes + 8, m_v)
    clear(6 * (planes + 6), s0_v)
    clear(6 * (planes + 4), s1_v)
    clear(6 * (planes + 2), u_v)

    lane = lax.broadcasted_iota(jnp.int32, (8, 128), 1)
    first_lane, last_lane = lane == 0, lane == 127

    def above(a):
        r0, r1 = pltpu.roll(a[0], 127, 1), pltpu.roll(a[1], 127, 1)
        return [jnp.where(last_lane, r1, r0), r1]

    def below(a):
        r0, r1 = pltpu.roll(a[0], 1, 1), pltpu.roll(a[1], 1, 1)
        return [r0, jnp.where(first_lane, r0, r1)]

    def get(ref, i, row):
        return [ref[i, z, pl.ds(row, 8), :] for z in range(2)]

    def moduli(own, at, count, ok):
        def plane(p):
            def put(source, r, row):
                for z in range(2):
                    d = source[p, pl.ds(r, 8), pl.ds(128 * z, 128)]
                    m_v[at + p, z, pl.ds(pl.multiple_of(PAD + row, 8), 8), :] = (E_MIN + d * d * d * (1.0 - E_MIN)) * ok

            def put_edge(p):
                for z in range(2):
                    d = edge_v[at + p, :, pl.ds(128 * z, 128)]
                    m_v[at + p, z, pl.ds(pl.multiple_of(PAD + (1 - h) * half, 8), 8), :] = (E_MIN + d * d * d * (1.0 - E_MIN)) * ok

            over_rows(half // 8, lambda r: put(own, r, skip + r))
            put_edge(p)

        over_planes(count, plane)

    def first(p, r, ok, index_at, support_at):
        r = pl.multiple_of(r, 8)
        row = pl.multiple_of(PAD + r, 8)
        m = get(m_v, p + 1, row)
        zup, zdn = above(m), below(m)
        zup[1] = jnp.where(last_lane, 0.0, zup[1])
        zdn[0] = jnp.where(first_lane, 0.0, zdn[0])
        beside = [get(m_v, p + 2, row), get(m_v, p, row), get(m_v, p + 1, row + 1), get(m_v, p + 1, row - 1), zup, zdn]
        stores = []
        for z in range(2):
            face = [m[z] + b[z] for b in beside]
            double = ((face[0] + face[1]) + (face[2] + face[3])) + (face[4] + face[5])
            diagonal = 0.5 * double + SPRING * support_at(z).astype(jnp.float32)
            w = ok / (diagonal + (1.0 - ok))
            wb = w * (0.5 * B1)
            weight = [f * wb for f in face]
            if z == 1:
                weight[4] = jnp.where(last_lane, 0.0, weight[4])
            else:
                weight[5] = jnp.where(first_lane, 0.0, weight[5])
            scale = w * (RATIO / CENTRE)
            for case in range(2):
                index = index_at(case, z)
                b0, b1, b2 = (index & 1) != 0, (index & 2) != 0, (index & 4) != 0
                forces = []
                for c in range(3):
                    q = [jnp.where(b0, table[2 * j + 1, c], table[2 * j, c]) for j in range(4)]
                    forces.append(jnp.where(b2, jnp.where(b1, q[3], q[2]), jnp.where(b1, q[1], q[0])))
                for c in range(3):
                    stores.append((s0_v, (p * 6 + case * 3 + c, z, pl.ds(row, 8)), forces[c] * scale))
            for j in range(6):
                stores.append((k_v, (p, j, z, pl.ds(r, 8)), weight[j]))
        for ref, at, value in stores:
            ref[at] = value

    def first_halo(source, side, at, ok):
        def from_source(p, refs, r, row):
            def cut(i, z):
                at = (i, pl.ds(pl.multiple_of(r, 8), 8), pl.ds(128 * z, 128))
                return refs[0][at] if len(refs) == 1 else refs[0][at] + refs[1][at]

            first(at + p, row, ok, lambda case, z: cut(3 * case + p, z), lambda z: cut(6 + p, z))

        def plane(p):
            if lo_s is None:
                over_rows(tiles, lambda r: from_source(p, (source,), r, r))
            else:
                over_rows(fresh // 8, lambda r: from_source(p, (source, (lo_l, hi_l)[side]), r, h * common + r))
                over_rows(common // 8, lambda r: from_source(p, ((lo_s, hi_s)[side],), r, (1 - h) * fresh + r))

        over_planes(3, plane)

    def first_own(p):
        def body(r):
            first(
                p + 3, r, 1.0,
                lambda case, z: idx_v[case, p, pl.ds(r, 8), pl.ds(128 * z, 128)],
                lambda z: sup_v[p, pl.ds(r, 8), pl.ds(128 * z, 128)])

        over_rows(tiles, body)

    def stencil(ref, at, row, k):
        c = get(ref, at, row)
        parts = [get(ref, at + 6, row), get(ref, at - 6, row), get(ref, at, row + 1), get(ref, at, row - 1), above(c), below(c)]
        out = []
        for z in range(2):
            t = [k[j][z] * parts[j][z] for j in range(6)]
            out.append(((t[0] + t[1]) + (t[2] + t[3])) + (t[4] + t[5]))
        return c, out

    def second(p):
        def body(r):
            row = PAD + r
            k = [[k_v[p + 1, j, z, pl.ds(r, 8), :] for z in range(2)] for j in range(6)]
            new = []
            for f in range(6):
                c, t = stencil(s0_v, (p + 1) * 6 + f, row, k)
                new.append([G0 * c[z] + t[z] for z in range(2)])
            for f in range(6):
                for z in range(2):
                    s1_v[p * 6 + f, z, pl.ds(row, 8), :] = new[f][z]

        over_rows(tiles, body)

    def third(p):
        def body(r):
            row = PAD + r
            k = [[k_v[p + 2, j, z, pl.ds(r, 8), :] for z in range(2)] for j in range(6)]
            new = []
            for f in range(6):
                c, t = stencil(s1_v, (p + 1) * 6 + f, row, k)
                base = get(s0_v, (p + 2) * 6 + f, row)
                new.append([(A0 / RATIO) * base[z] + (A1 / RATIO) * c[z] + t[z] for z in range(2)])
            for f in range(6):
                for z in range(2):
                    u_v[p * 6 + f, z, pl.ds(row, 8), :] = new[f][z]

        over_rows(tiles, body)

    def out_copies(p):
        return [
            pltpu.make_async_copy(
                u_v.at[(p + 1) * 6 + f, z, pl.ds(PAD + skip, half), :],
                u_out.at[f // 3, f % 3, p, pl.ds(pl.multiple_of(h * half, 8), half), pl.ds(128 * z, 128)],
                out_sem.at[p * 12 + f * 2 + z])
            for f in range(6) for z in range(2)
        ]

    def energy(p):
        def body(r):
            row = PAD + r
            acc = [[], []]
            for f in range(6):
                at = (p + 1) * 6 + f
                c = get(u_v, at, row)
                zup, zdn = above(c), below(c)
                zup[1] = jnp.where(last_lane, 0.0, zup[1])
                zdn[0] = jnp.where(first_lane, 0.0, zdn[0])
                for b in (get(u_v, at + 6, row), get(u_v, at - 6, row), get(u_v, at, row + 1), get(u_v, at, row - 1), zup, zdn):
                    for z in range(2):
                        d = c[z] - b[z]
                        if len(acc[z]) < 3:
                            acc[z].append(d * d)
                        else:
                            acc[z] = acc[z][1:] + [acc[z][0] + d * d]
            for z in range(2):
                e_out[p, pl.ds(r, 8), pl.ds(128 * z, 128)] = 0.5 * (acc[z][0] + acc[z][1] + acc[z][2])

        over_rows(tiles, body)

    moduli(lo_d, 0, 4, vlo)
    moduli(mid, 4, planes, 1.0)
    moduli(hi_d, planes + 4, 4, vhi)
    first_halo(lo_i, 0, 0, vlo)
    first_halo(hi_i, 1, planes + 3, vhi)
    for copy in owned:
        copy.wait()
    over_planes(planes, first_own)
    over_planes(planes + 4, second)
    over_planes(planes + 2, third)
    for p in range(planes):
        for copy in out_copies(p):
            copy.start()
    over_planes(planes, energy)
    for p in range(planes):
        for copy in out_copies(p):
            copy.wait()


def step(h, gap, valid, table, loads, support, main, edge, ints, u):
    planes, half, cols = main[1].shape
    rows = half + EXTRA
    tiles_rows = rows + 2 * PAD
    f32 = jnp.float32
    any_spec = pl.BlockSpec(memory_space=pl.ANY)
    smem = pl.BlockSpec(memory_space=pltpu.SMEM)
    vmem = pl.BlockSpec(memory_space=pltpu.VMEM)
    full = loads.shape[2]
    args = [jnp.stack([h, gap]).astype(jnp.int32), table, valid, loads, support, *main, edge, *ints]
    specs = [smem] * 3 + [pl.BlockSpec(memory_space=pltpu.HBM)] * 2 + [vmem] * (len(args) - 5)
    aliases = {}
    if u is not None:
        args.append(u)
        specs.append(any_spec)
        aliases = {len(args) - 1: 0}

    def kernel(*refs):
        step_kernel(planes, rows, *refs)

    return pl.pallas_call(
        kernel,
        out_shape=(jax.ShapeDtypeStruct((2, 3, planes, full, cols), f32), jax.ShapeDtypeStruct((planes, rows, cols), f32)),
        in_specs=specs,
        out_specs=(any_spec, vmem),
        input_output_aliases=aliases,
        scratch_shapes=[
            pltpu.VMEM((2, planes, rows, cols), jnp.int32),
            pltpu.VMEM((planes, rows, cols), jnp.int32),
            pltpu.VMEM((planes + 8, 2, tiles_rows, 128), f32),
            pltpu.VMEM((planes + 6, 6, 2, rows, 128), f32),
            pltpu.VMEM((6 * (planes + 6), 2, tiles_rows, 128), f32),
            pltpu.VMEM((6 * (planes + 4), 2, tiles_rows, 128), f32),
            pltpu.VMEM((6 * (planes + 2), 2, tiles_rows, 128), f32),
            pltpu.SemaphoreType.DMA((3,)),
            pltpu.SemaphoreType.DMA((12 * planes,)),
        ],
        compiler_params=pltpu.CompilerParams(vmem_limit_bytes=42 * 1024 * 1024),
        cost_estimate=pl.CostEstimate(flops=40_000_000, bytes_accessed=40_000_000, transcendentals=0),
        name="relax",
    )(*args)


def filter_kernel(planes, rows, info, valid, lo, mid, hi, dens, out, r_v, a_v, b_v):
    tiles = rows // 8
    h = info[0]
    vlo, vhi = valid[0], valid[1]
    half = rows - EXTRA
    zero = jnp.zeros((PAD, 128), jnp.float32)
    lane = lax.broadcasted_iota(jnp.int32, (8, 128), 1)
    first_lane, last_lane = lane == 0, lane == 127

    def clear(i, carry):
        for ref in (r_v, a_v, b_v):
            for z in range(2):
                ref[i, z, pl.ds(0, PAD), :] = zero
                ref[i, z, pl.ds(PAD + rows, PAD), :] = zero
        return carry

    lax.fori_loop(0, planes + 8, clear, 0, unroll=4)

    def batches(total, body):
        for at in range(0, total, 5):
            body([8 * j for j in range(at, min(at + 5, total))])

    def fill(source, at, count):
        def plane(p, carry):
            def body(offsets):
                new = [[source[p, pl.ds(r, 8), pl.ds(128 * z, 128)] for z in range(2)] for r in offsets]
                for r, v in zip(offsets, new):
                    for z in range(2):
                        r_v[at + p, z, pl.ds(PAD + r, 8), :] = v[z]

            batches(tiles, body)
            return carry

        lax.fori_loop(0, count, plane, 0)

    fill(lo, 0, 4)
    fill(mid, 4, planes)
    fill(hi, planes + 4, 4)

    def smoothed(src, p, row, scale):
        c = [src[p, z, pl.ds(row, 8), :] for z in range(2)]
        u0, u1 = pltpu.roll(c[0], 127, 1), pltpu.roll(c[1], 127, 1)
        d0, d1 = pltpu.roll(c[0], 1, 1), pltpu.roll(c[1], 1, 1)
        zs = [
            jnp.where(last_lane, u1, u0) + jnp.where(first_lane, 0.0, d0),
            jnp.where(last_lane, 0.0, u1) + jnp.where(first_lane, d0, d1),
        ]
        new = []
        for z in range(2):
            total = (src[p + 1, z, pl.ds(row, 8), :] + src[p - 1, z, pl.ds(row, 8), :]) + (
                src[p, z, pl.ds(row + 1, 8), :] + src[p, z, pl.ds(row - 1, 8), :]) + zs[z]
            new.append((r_v[p, z, pl.ds(row, 8), :] + RADIUS_SQ * total) * scale)
        return new

    def sweep(src, dst, low, high):
        def plane(i, carry):
            p = low + i
            ok = jnp.where(p < 4, vlo, jnp.where(p >= planes + 4, vhi, 1.0))
            scale = ok * (1.0 / (1.0 + 6.0 * RADIUS_SQ))

            def body(offsets):
                new = [smoothed(src, p, pl.multiple_of(PAD + r, 8) if not isinstance(r, int) else PAD + r, scale) for r in offsets]
                for r, v in zip(offsets, new):
                    for z in range(2):
                        dst[p, z, pl.ds(PAD + r, 8), :] = v[z]

            batches(tiles, body)
            return carry

        lax.fori_loop(0, high - low, plane, 0)

    sweep(r_v, a_v, 1, planes + 7)
    sweep(a_v, b_v, 2, planes + 6)
    sweep(b_v, a_v, 3, planes + 5)

    skip = pl.multiple_of(h * EXTRA, 8)

    def last(p, carry):
        def body(offsets):
            new = [smoothed(a_v, p + 4, pl.multiple_of(PAD + r + skip, 8), 1.0 / (1.0 + 6.0 * RADIUS_SQ)) for r in offsets]
            for r, v in zip(offsets, new):
                for z in range(2):
                    out[p, pl.ds(r, 8), pl.ds(128 * z, 128)] = v[z] / dens[p, pl.ds(r, 8), pl.ds(128 * z, 128)]

        batches(half // 8, body)
        return carry

    lax.fori_loop(0, planes, last, 0)


def smooth(h, gap, valid, lo, mid, hi, dens):
    planes, rows, cols = mid.shape
    f32 = jnp.float32
    smem = pl.BlockSpec(memory_space=pltpu.SMEM)
    vmem = pl.BlockSpec(memory_space=pltpu.VMEM)

    def kernel(*refs):
        filter_kernel(planes, rows, *refs)

    return pl.pallas_call(
        kernel,
        out_shape=jax.ShapeDtypeStruct(dens.shape, f32),
        in_specs=[smem, smem] + [vmem] * 4,
        out_specs=vmem,
        scratch_shapes=[pltpu.VMEM((planes + 8, 2, rows + 2 * PAD, 128), f32)] * 3,
        compiler_params=pltpu.CompilerParams(vmem_limit_bytes=32 * 1024 * 1024),
        cost_estimate=pl.CostEstimate(flops=5_000_000, bytes_accessed=5_000_000, transcendentals=0),
        name="smooth",
    )(jnp.stack([h, gap]).astype(jnp.int32), valid, lo, mid, hi, dens)


def local(density, support, loads, load_table):
    planes, half, cols = density.shape
    full = loads.shape[2]
    rows = half + EXTRA
    gap = full - rows
    mine = lax.axis_index("case")
    count = lax.axis_size("slab")
    at = lax.axis_index("slab")
    valid = jnp.stack([at > 0, at < count - 1]).astype(jnp.float32)
    rise = [(i, i + 1) for i in range(count - 1)]
    fall = [(i + 1, i) for i in range(count - 1)]
    swap = [(0, 1), (1, 0)]

    partner = lax.ppermute(density, "case", swap)
    lo_c = lax.ppermute(density[planes - 4:], "slab", rise)
    hi_c = lax.ppermute(density[:4], "slab", fall)

    def packed(start, length):
        own = lax.dynamic_slice_in_dim(loads, start, length, axis=2)
        sup = lax.dynamic_slice_in_dim(support, start, length, axis=1)

        def pack(a, b):
            return jnp.concatenate([own[0, a:b], own[1, a:b], sup[a:b]], axis=0)

        return pack(planes - 3, planes), pack(0, 3)

    def exchange(up, down, keep=lambda i: True):
        return (
            lax.ppermute(up, "slab", [pair for pair in rise if keep(pair[1])]),
            lax.ppermute(down, "slab", [pair for pair in fall if keep(pair[0])]),
        )

    payload_a = packed((1 - mine) * gap, rows)
    payload_b = packed(mine * rows, rows - 2 * EXTRA)
    ints_a = exchange(*payload_a)
    lo_c, hi_c, partner, _ = lax.optimization_barrier((lo_c, hi_c, partner, payload_a))
    both = lax.ppermute(jnp.concatenate([lo_c, hi_c]), "case", swap)
    both, payload_b = lax.optimization_barrier((both, payload_b))
    lo_o, hi_o = both[:4], both[4:]
    common = [lax.dynamic_slice_in_dim(v, mine * (rows - 2 * EXTRA), 2 * EXTRA, axis=1) for v in ints_a]
    ints_b = (*exchange(*payload_b, lambda i: i % 4), *common)
    ints_a, late = lax.optimization_barrier((ints_a, payload_b))
    ints_b += exchange(*late, lambda i: i % 4 == 0)
    own = (lo_c, density, hi_c)
    opposite = (lo_o, partner, hi_o)

    def edge(h, parts):
        return jnp.concatenate([lax.dynamic_slice_in_dim(v, h * (half - EXTRA), EXTRA, axis=1) for v in parts])

    u, e_a = step(1 - mine, gap, valid, load_table, loads, support, opposite, edge(1 - mine, own), ints_a, None)
    received = lax.ppermute(e_a, "case", swap)
    u, e_b = step(mine, gap, valid, load_table, loads, support, own, edge(mine, opposite), ints_b, u)
    low = jnp.concatenate([density, partner[:, :EXTRA]], axis=1)
    high = jnp.concatenate([partner[:, half - EXTRA:], density], axis=1)
    mid = jnp.where(mine == 0, low, high)
    right = (-PENALTY * (1.0 - E_MIN)) * (mid * mid * mid) * (e_b + received)
    lo_r, hi_r = exchange(right[planes - 4:], right[:4])
    filtered = smooth(mine, gap, valid, lo_r, right, hi_r, density)
    return u, filtered


def solution(mesh):
    return jax.shard_map(
        local,
        mesh=mesh,
        in_specs=(
            P("slab", "case", None),
            P("slab", None, None),
            P("case", "slab", None, None),
            P(),
        ),
        out_specs=(P("case", None, "slab", None, None), P("slab", "case", None)),
        check_vma=False,
    )
```
